32 devices in a mesh: tm: 8 (over z, y), table: 4 (over x, core).
Axes of the slice: x: 2, y: 2, z: 4, core: 2. Of those that a mesh axis runs over, the one named last changes fastest.
Arguments:
- out_grad: bfloat16 [4, 16384, 512], P('table', 'tm'), may hold values from -1.1953125 to 1.1953125
- bc_proj: bfloat16 [4, 16384, 128], P('table', 'tm'), may hold values from -0.18847656 to 0.18847656
- decay_log: float32 [4, 8, 16384], P('table', None, 'tm'), may hold values from -1 to 0
- skip_gain: float32 [8], replicated, may hold values from 0.5 to 1.5
- owner: int32 [4, 16384, 1], P('table', 'tm'), may hold values from 0 to 31; in each aligned block of 2048 rows (0 to 2047, 2048 to 4095, ..., all dimensions but the last counted through in order) at most 128 rows name the same one
- item_row: int32 [4, 16384], P('table', 'tm'), may hold values from 0 to 1535
- table: bfloat16 [49152, 512], P(('tm', 'table')), may hold values from -3 to 3
- accum: float32 [49152, 512], P(('tm', 'table')), may hold values from 1 to 10
Outputs:
- new_table: bfloat16 [49152, 512], P(('tm', 'table'))
- new_accum: float32 [49152, 512], P(('tm', 'table'))
The draws below stay inside these ranges and needn't reach their ends.
Inputs may be any that keep to these rules, and one draw needn't show every extreme that they name: Among the events of one device at most 128 have the same owner; in every draw some device has exactly 128 events for some owner.
All inputs are finite; a program needn't handle non-finite values.
Results may differ from the reference program's by a relative error of at most 0.0018.
Values may be sent and summed in bfloat16 or wider, within the bound.
No kernel may reach another device: no remote copies, remote signals or barrier semaphores. Data moves between devices by JAX's collectives and lax.ppermute only.
A program may use at most 128 MiB of HBM per device.

```python
import math
import jax
import jax.numpy as jnp
import numpy as np
from jax import lax

D = 512
HEADS = 8
HEAD_DIM = 64
STATE = 64
GROUP = 256
EV_DEV = 2048
USR_DEV = 1
V_OWN = 1536
EVENT_LENGTH = 16384
USER_COUNT = 4
ITEMS = 49152
CAP = 128
DEVICES = 32


def draw_decay_log(key, part):
    random_keys = jax.random.split(key, 7)
    fast_share = 0.5
    fast = jax.random.bernoulli(random_keys[0], fast_share, (USER_COUNT, HEADS, 1)).astype(jnp.float32)
    fast_rate = jnp.exp(jax.random.uniform(random_keys[1], (USER_COUNT, HEADS, 1), jnp.float32, math.log(1.0 / 50.0), math.log(1.0 / 30.0)))
    slow_rate = 0.5 / EVENT_LENGTH * jax.random.uniform(random_keys[2], (USER_COUNT, HEADS, 1), jnp.float32, 0.5, 1.0)
    baseline_value = fast * fast_rate + (1.0 - fast) * slow_rate
    approximate_value = jnp.exp(jax.random.uniform(random_keys[3], (USER_COUNT, HEADS, EVENT_LENGTH), jnp.float32, -0.7, 0.7))
    approximate_grid = jnp.exp(jax.random.uniform(random_keys[4], (USER_COUNT, HEADS, EVENT_LENGTH // GROUP), jnp.float32, -0.7, 0.7))
    approximate_grid = jnp.repeat(approximate_grid, GROUP, axis=2)
    spike_position = jax.random.bernoulli(random_keys[5], 4.0 / EVENT_LENGTH, (USER_COUNT, 1, EVENT_LENGTH)).astype(jnp.float32)
    spike_events = spike_position * jnp.log(jax.random.uniform(random_keys[6], (USER_COUNT, 1, EVENT_LENGTH), jnp.float32, 0.5, 0.8))
    return -baseline_value * approximate_value * approximate_grid + spike_events


def place_ends(array, key, least, top_value):
    longest = array.shape.index(max(array.shape))
    spots = []
    for shift in (0, 1):
        where = [jax.random.randint(jax.random.fold_in(key, axis), (), 0, length) for axis, length in enumerate(array.shape)]
        where[longest] = (where[longest] + shift) % array.shape[longest]
        spots.append(tuple(where))
    return array.at[spots[0]].set(least).at[spots[1]].set(top_value)


def steps_of(stream_key, shape, pieces, least, largest):
    level, own = 1.0, jax.random.fold_in(stream_key, 6)
    for dim, blocks in pieces:
        heights = jnp.exp(jax.random.uniform(jax.random.fold_in(own, dim), (blocks,), jnp.float32, least / len(pieces), largest / len(pieces)))
        level = level * jnp.repeat(heights, shape[dim] // blocks).reshape([-1 if axis == dim else 1 for axis in range(len(shape))])
    return level


def routed_block(own_key, own, number, rows, count, top, bound, slope):
    sequence = jax.random.permutation(own_key, count)
    crowded, ordinary = portions_of(count, rows * top, bound, slope, True), portions_of(count, rows * top, bound, slope, False)
    places = jnp.arange(count)

    def named(lengths, rotation):
        used = int((lengths > 0).sum())
        fixed = max(1, used // 4)
        shifted = fixed + (places - fixed + rotation * (used - fixed)) % max(1, count - fixed)
        return jnp.zeros((count,), jnp.int32).at[sequence[jnp.where(places < fixed, places, shifted)]].set(jnp.asarray(lengths, jnp.int32))

    lengths = jnp.where(number % 4 == 0, named(crowded, number // 4), named(ordinary, number - number // 4 - 1))
    mixed = jax.random.permutation(jax.random.fold_in(own, 3), count)
    source_of, sink = mixed[0:count // 2 * 2:2], mixed[1:count // 2 * 2:2]
    room = jnp.minimum(lengths[source_of] - 1, bound - lengths[sink]) // 2
    room = jnp.where((source_of == sequence[0]) | (sink == sequence[0]) | (lengths[sink] == 0), 0, jnp.maximum(room, 0))
    shifted = jax.random.randint(jax.random.fold_in(own, 4), (count // 2,), 0, 1 << 20) % (room + 1)
    lengths = lengths.at[source_of].add(-shifted).at[sink].add(shifted)
    members = jnp.searchsorted(jnp.cumsum(lengths), jnp.arange(rows * top), side="right").astype(jnp.int32)
    grid = members.reshape(top, rows).T
    grid = grid[jax.random.permutation(jax.random.fold_in(own, 1), rows)]
    rotation = jax.random.randint(jax.random.fold_in(own, 2), (rows, 1), 0, top)
    return jnp.take_along_axis(grid, (jnp.arange(top)[None, :] + rotation) % top, axis=1)


def portions_of(count, total, most, slope, full):
    weights = [(1 << 20) // math.isqrt(standing ** slope) + 1 for standing in range(1, count + 1)]
    largest = most if full else min(most, max(-(-total // count), total * weights[0] // sum(weights)))
    least = 1 if total - largest >= count - 1 else 0
    given, spare = [largest] + [least] * (count - 1), total - largest - least * (count - 1)
    while spare > 0:
        movable = [i for i in range(1, count) if given[i] < largest] or [i for i in range(1, count) if given[i] < most]
        whole, left = sum([weights[i] for i in movable]), spare
        for i in movable:
            extra = min(most - given[i], max(1, left * weights[i] // whole), spare)
            given[i] = given[i] + extra
            spare = spare - extra
    return np.array(given)


def centred(own_key, dims, width, reach, cuts=(), held_as=jnp.bfloat16):
    entries = width * jax.random.normal(own_key, dims, jnp.float32)
    if cuts:
        entries = entries * steps_of(own_key, dims, cuts, -0.22, 0.18)
    return jnp.clip(entries, -reach, reach).astype(held_as)


def setup_inputs(seed: int = 0) -> dict:
    keys = jax.random.split(jax.random.key(seed), 9)
    out_grad = centred(keys[0], (USER_COUNT, EVENT_LENGTH, D), 0.2, 1.1953125, ((0, 4), (1, 8)))
    bc_proj = centred(keys[1], (USER_COUNT, EVENT_LENGTH, 2 * STATE), (0.6 / (EV_DEV * STATE) ** 0.25), 0.18847656, ((0, 4), (1, 8)))
    decay_log = draw_decay_log(jax.random.fold_in(keys[8], 71), 0)
    skip_gain = jnp.clip(jax.random.uniform(keys[3], (HEADS,), jnp.float32, 0.5, 1.5), 0.5, 1.5)
    owner_keys = jax.random.split(jax.random.fold_in(keys[4], 1), USER_COUNT * EVENT_LENGTH // (USR_DEV * EV_DEV))
    owner_turns = jax.random.permutation(jax.random.fold_in(keys[4], 3), USER_COUNT * EVENT_LENGTH // (USR_DEV * EV_DEV))
    owner = jax.vmap(lambda own, number: routed_block(jax.random.fold_in(keys[4], 2), own, number, USR_DEV * EV_DEV, DEVICES, 1, CAP, 2))(owner_keys, owner_turns).reshape((USER_COUNT, EVENT_LENGTH, 1))
    item_row = place_ends(jax.random.randint(keys[5], (USER_COUNT, EVENT_LENGTH), 0, V_OWN), jax.random.fold_in(keys[5], 1), 0, V_OWN - 1).astype(jnp.int32)
    table = centred(keys[6], (ITEMS, D), 0.5, 3.0, ((0, 32),))
    accum = jnp.clip(jnp.exp(math.log(10.0) - 2.3025851 * jax.random.uniform(keys[7], (ITEMS, D), jnp.float32) ** steps_of(keys[7], (ITEMS, D), ((0, 32),), -0.2, 0.2)), 1.0, 10.0)
    return dict(out_grad=out_grad, bc_proj=bc_proj, decay_log=decay_log, skip_gain=skip_gain, owner=owner, item_row=item_row, table=table, accum=accum)


learn_rate = 1.0

def block_end(grad_block, c_block, decay_block):
    cumul = jnp.cumsum(decay_block, axis=1)
    length = grad_block.shape[0]
    scaled = grad_block.astype(jnp.float32).reshape(length, HEADS, -1) * jnp.exp(cumul).T[:, :, None]
    ends = jnp.einsum('thp,tn->hpn', scaled, c_block.astype(jnp.float32), precision=lax.Precision.HIGHEST)
    return (cumul[:, -1], ends)

def fold_back(carry, item):
    log_end, end_term = item
    return (end_term + jnp.exp(log_end)[:, None, None] * carry, carry)

def block_rows(grad_block, b_block, c_block, decay_block, carried, skip_gain):
    length = grad_block.shape[0]
    cumul = jnp.cumsum(decay_block, axis=1)
    scores = jnp.dot(c_block, b_block.T, preferred_element_type=jnp.float32)
    later = jnp.arange(length)[:, None] >= jnp.arange(length)[None, :]
    gaps = jnp.where(later[None], cumul[:, :, None] - cumul[:, None, :], 0.0)
    mixing = jnp.where(later[None], jnp.exp(gaps) * scores[None], 0.0).astype(jnp.bfloat16)
    heads_grad = grad_block.reshape(length, HEADS, -1)
    inner = jnp.einsum('hts,thp->shp', mixing.astype(jnp.float32), heads_grad.astype(jnp.float32))
    fading = jnp.exp(cumul[:, -1:] - cumul)
    carried_part = jnp.einsum('hpn,sn->shp', carried, b_block.astype(jnp.float32), precision=lax.Precision.HIGHEST) * fading.T[:, :, None]
    total = inner + carried_part + skip_gain[None, :, None] * heads_grad.astype(jnp.float32)
    return total.reshape(length, -1).astype(jnp.bfloat16)

def reference(out_grad, bc_proj, decay_log, skip_gain, owner, item_row, table, accum):
    blocks = EVENT_LENGTH // GROUP
    item = (owner[:, :, 0] * V_OWN + item_row).astype(jnp.int32)

    def user_step(total, inputs):
        grad_user, bc_user, decay_user, item_user = inputs
        grad_blocks = grad_user.reshape(blocks, GROUP, D)
        b_blocks = bc_user[:, :STATE].reshape(blocks, GROUP, STATE)
        c_blocks = bc_user[:, STATE:].reshape(blocks, GROUP, STATE)
        decay_blocks = decay_user.reshape(HEADS, blocks, GROUP).transpose(1, 0, 2)
        log_ends, end_terms = lax.map(lambda a: block_end(a[0], a[1], a[2]), (grad_blocks, c_blocks, decay_blocks))
        start = jnp.zeros((HEADS, HEAD_DIM, STATE), jnp.float32)
        _, carried = lax.scan(fold_back, start, (log_ends, end_terms), reverse=True)
        rows = lax.map(lambda a: block_rows(a[0], a[1], a[2], a[3], a[4], skip_gain), (grad_blocks, b_blocks, c_blocks, decay_blocks, carried))
        total = total.at[item_user].add(rows.reshape(EVENT_LENGTH, D).astype(jnp.float32))
        return (total, 0)
    zeros = jnp.zeros((ITEMS, D), jnp.float32)
    item_grad, _ = lax.scan(user_step, zeros, (out_grad, bc_proj, decay_log, item))
    new_accum = accum + item_grad * item_grad
    new_table = (table.astype(jnp.float32) - learn_rate * item_grad / jnp.sqrt(new_accum)).astype(jnp.bfloat16)
    return (new_table, new_accum)
```

```python
import functools

import jax
import jax.numpy as jnp
from jax import lax
from jax.experimental import pallas as pl
from jax.experimental.pallas import tpu as pltpu
from jax.sharding import PartitionSpec as P

HEADS = 8
STATE = 64
GROUP = 256
BOTH = ("tm", "table")
VMEM_BYTES = 48 * 1024 * 1024

learn_rate = 1.0

f32 = jnp.float32
bf16 = jnp.bfloat16
HIGHEST = lax.Precision.HIGHEST


def params():
    return pltpu.CompilerParams(vmem_limit_bytes=VMEM_BYTES)


def cost(flops, moved, exps=0):
    return pl.CostEstimate(flops=flops, bytes_accessed=moved, transcendentals=exps)


def spread(columns, width):
    rows = columns.shape[0]
    head_dim = width // HEADS
    low = lax.broadcasted_iota(jnp.int32, (rows, 2 * head_dim), 1) < head_dim
    parts = [
        jnp.where(low, columns[:, h : h + 1], columns[:, h + 1 : h + 2]) for h in range(0, HEADS, 2)
    ]
    return jnp.concatenate(parts, axis=1)


def cumul_columns(decay):
    shape = (GROUP, GROUP)
    upto = (lax.broadcasted_iota(jnp.int32, shape, 1) <= lax.broadcasted_iota(jnp.int32, shape, 0))
    return lax.dot_general(
        jnp.where(upto, 1.0, 0.0), decay, (((1,), (1,)), ((), ())), precision=HIGHEST,
        preferred_element_type=f32,
    )


def cumul_rows(decay):
    shape = (GROUP, GROUP)
    upto = (lax.broadcasted_iota(jnp.int32, shape, 0) <= lax.broadcasted_iota(jnp.int32, shape, 1))
    return jnp.dot(
        decay, jnp.where(upto, 1.0, 0.0), precision=HIGHEST, preferred_element_type=f32
    )


def two_parts(x):
    high = x.astype(bf16)
    return high, (x - high.astype(f32)).astype(bf16)


def state_kernel(grad_ref, bc_ref, decay_ref, carried_ref, after_ref, end_ref, log_ref, state, log):
    width = grad_ref.shape[1]

    @pl.when(pl.program_id(0) == 0)
    def _():
        state[...] = jnp.zeros_like(state)
        log[...] = jnp.zeros_like(log)

    cumul = cumul_columns(decay_ref[...])
    scaled = grad_ref[...].astype(f32) * spread(jnp.exp(cumul), width)
    c = bc_ref[:, STATE:]
    high, low = two_parts(scaled)
    dims = (((0,), (0,)), ((), ()))
    ends = lax.dot_general(c, high, dims, preferred_element_type=f32) + lax.dot_general(
        c, low, dims, preferred_element_type=f32
    )
    carried_ref[0] = state[...]
    after_ref[0] = log[...]
    log_end = spread(cumul[GROUP - 1 :, :], width)
    state[...] = ends + jnp.exp(log_end) * state[...]
    log[...] = log[...] + log_end
    end_ref[...] = state[...]
    log_ref[...] = log[...]


def state_of(grad, bc, decay):
    events, width = grad.shape
    blocks = events // GROUP
    back = lambda i: (blocks - 1 - i, 0)
    return pl.pallas_call(
        state_kernel,
        grid=(blocks,),
        in_specs=[
            pl.BlockSpec((GROUP, width), back),
            pl.BlockSpec((GROUP, 2 * STATE), back),
            pl.BlockSpec((HEADS, GROUP), lambda i: (0, blocks - 1 - i)),
        ],
        out_specs=[
            pl.BlockSpec((1, STATE, width), lambda i: (blocks - 1 - i, 0, 0)),
            pl.BlockSpec((1, 1, width), lambda i: (blocks - 1 - i, 0, 0)),
            pl.BlockSpec((STATE, width), lambda i: (0, 0)),
            pl.BlockSpec((1, width), lambda i: (0, 0)),
        ],
        out_shape=[
            jax.ShapeDtypeStruct((blocks, STATE, width), f32),
            jax.ShapeDtypeStruct((blocks, 1, width), f32),
            jax.ShapeDtypeStruct((STATE, width), f32),
            jax.ShapeDtypeStruct((1, width), f32),
        ],
        scratch_shapes=[pltpu.VMEM((STATE, width), f32), pltpu.VMEM((1, width), f32)],
        compiler_params=params(),
        cost_estimate=cost(4 * events * width * STATE, 4 * events * width),
        name="state",
    )(grad, bc, decay)


def local_kernel(grad_ref, bc_ref, decay_ref, skip_ref, carried_ref, after_ref, out_ref, fade_ref):
    width = grad_ref.shape[1]
    head_dim = width // HEADS
    decay = decay_ref[...]
    columns, rows = cumul_columns(decay), cumul_rows(decay)
    b, c = bc_ref[:, :STATE], bc_ref[:, STATE:]
    scores = lax.dot_general(b, c, (((1,), (1,)), ((), ())), preferred_element_type=f32)
    shape = (GROUP, GROUP)
    later = lax.broadcasted_iota(jnp.int32, shape, 1) >= lax.broadcasted_iota(jnp.int32, shape, 0)
    scores = jnp.where(later, scores, 0.0)
    grad = grad_ref[...]
    inner = []
    for h in range(HEADS):
        gaps = jnp.where(later, rows[h : h + 1, :] - columns[:, h : h + 1], 0.0)
        mixing = (jnp.exp(gaps) * scores).astype(bf16)
        inner.append(
            jnp.dot(
                mixing, grad[:, h * head_dim : (h + 1) * head_dim], preferred_element_type=f32
            )
        )
    fading = spread(jnp.exp(columns[GROUP - 1 :, :] - columns), width)
    high, low = two_parts(carried_ref[0])
    carried = jnp.dot(b, high, preferred_element_type=f32) + jnp.dot(
        b, low, preferred_element_type=f32
    )
    gain = spread(skip_ref[...], width)
    out_ref[...] = jnp.concatenate(inner, axis=1) + carried * fading + gain * grad.astype(f32)
    fade_ref[...] = fading * jnp.exp(after_ref[0])


def local_rows(grad, bc, decay, skip, carried, after):
    events, width = grad.shape
    blocks = events // GROUP
    at = lambda i: (i, 0)
    return pl.pallas_call(
        local_kernel,
        grid=(blocks,),
        in_specs=[
            pl.BlockSpec((GROUP, width), at),
            pl.BlockSpec((GROUP, 2 * STATE), at),
            pl.BlockSpec((HEADS, GROUP), lambda i: (0, i)),
            pl.BlockSpec((1, HEADS), lambda i: (0, 0)),
            pl.BlockSpec((1, STATE, width), lambda i: (i, 0, 0)),
            pl.BlockSpec((1, 1, width), lambda i: (i, 0, 0)),
        ],
        out_specs=[pl.BlockSpec((GROUP, width), at), pl.BlockSpec((GROUP, width), at)],
        out_shape=[jax.ShapeDtypeStruct((events, width), f32)] * 2,
        compiler_params=params(),
        cost_estimate=cost(
            blocks * GROUP * GROUP * (2 * width + 8 * HEADS), 10 * events * width,
            blocks * GROUP * GROUP * HEADS,
        ),
        name="local",
    )(grad, bc, decay, skip, carried, after)


def slots_kernel(capacity, owner_ref, row_ref, place_ref, ids_ref):
    holders = ids_ref.shape[0]
    shape = (GROUP, GROUP)
    before = lax.broadcasted_iota(jnp.int32, shape, 0) < lax.broadcasted_iota(jnp.int32, shape, 1)
    before = jnp.where(before, 1.0, 0.0).astype(bf16)
    count = jnp.zeros((holders, 1), f32)
    names = lax.broadcasted_iota(jnp.int32, (holders, GROUP), 0)
    ranks = lax.broadcasted_iota(jnp.int32, (capacity, GROUP), 0)
    high = jnp.zeros((holders, capacity), f32)
    low = jnp.zeros((holders, capacity), f32)
    across = (((1,), (1,)), ((), ()))
    for k in range(owner_ref.shape[0]):
        target = owner_ref[k : k + 1, :]
        hit = names == target
        hits = jnp.where(hit, 1.0, 0.0)
        earlier = jnp.dot(hits.astype(bf16), before, preferred_element_type=f32) + count
        rank = jnp.sum(hits * earlier, axis=0, keepdims=True).astype(jnp.int32)
        count = count + jnp.sum(hits, axis=1, keepdims=True)
        place_ref[k : k + 1, :] = target * capacity + rank
        ranked = jnp.where(ranks == rank, 1.0, 0.0).astype(bf16)
        named = row_ref[k : k + 1, :] + 1
        upper = (hits * (named // 64).astype(f32)).astype(bf16)
        lower = (hits * (named % 64).astype(f32)).astype(bf16)
        high = high + lax.dot_general(upper, ranked, across, preferred_element_type=f32)
        low = low + lax.dot_general(lower, ranked, across, preferred_element_type=f32)
    ids_ref[...] = (high * 64.0 + low).astype(jnp.int32)


def slots(owner, row, holders, capacity):
    return pl.pallas_call(
        functools.partial(slots_kernel, capacity),
        out_shape=[
            jax.ShapeDtypeStruct(owner.shape, jnp.int32),
            jax.ShapeDtypeStruct((holders, capacity), jnp.int32),
        ],
        compiler_params=params(),
        cost_estimate=cost(2 * holders * owner.size * (GROUP + 2 * capacity), 8 * owner.size),
        name="slots",
    )(owner, row)


def send_kernel(tile, place_ref, bc_ref, local_ref, fade_ref, state_ref, out_ref, rows):
    step = pl.program_id(0)

    @pl.when(step == 0)
    def _():
        high, low = two_parts(state_ref[...])
        for k in range(place_ref.shape[0]):
            at = pl.ds(k * GROUP, GROUP)
            b = bc_ref[at, :STATE]
            part = jnp.dot(b, high, preferred_element_type=f32) + jnp.dot(
                b, low, preferred_element_type=f32
            )
            rows[at, :] = (local_ref[at, :] + part * fade_ref[at, :]).astype(bf16)

    places = lax.broadcasted_iota(jnp.int32, (tile, GROUP), 0) + step * tile
    total = jnp.zeros(out_ref.shape, f32)
    for k in range(place_ref.shape[0]):
        chosen = jnp.where(places == place_ref[k : k + 1, :], 1.0, 0.0).astype(bf16)
        total = total + jnp.dot(
            chosen, rows[pl.ds(k * GROUP, GROUP), :], preferred_element_type=f32
        )
    out_ref[...] = total.astype(bf16)


def sent_rows(place, bc, local, fade, state, places):
    events, width = local.shape
    tile = 512
    whole = lambda a: pl.BlockSpec(a.shape, lambda i: (0,) * a.ndim)
    return pl.pallas_call(
        functools.partial(send_kernel, tile),
        grid=(places // tile,),
        in_specs=[whole(place), whole(bc), whole(local), whole(fade), whole(state)],
        out_specs=pl.BlockSpec((tile, width), lambda i: (i, 0)),
        out_shape=jax.ShapeDtypeStruct((places, width), bf16),
        scratch_shapes=[pltpu.VMEM((events, width), bf16)],
        compiler_params=params(),
        cost_estimate=cost(2 * places * events * width, 12 * events * width),
        name="send",
    )(place, bc, local, fade, state)


def update_kernel(tile, ids_ref, got_ref, table_ref, accum_ref, new_table_ref, new_accum_ref):
    names = lax.broadcasted_iota(jnp.int32, (tile, GROUP), 0) + (pl.program_id(0) * tile + 1)
    total = jnp.zeros(accum_ref.shape, f32)
    for k in range(ids_ref.shape[0]):
        chosen = jnp.where(names == ids_ref[k : k + 1, :], 1.0, 0.0).astype(bf16)
        total = total + jnp.dot(
            chosen, got_ref[pl.ds(k * GROUP, GROUP), :], preferred_element_type=f32
        )
    accum = accum_ref[...] + total * total
    new_accum_ref[...] = accum
    new_table_ref[...] = (
        table_ref[...].astype(f32) - learn_rate * total / jnp.sqrt(accum)
    ).astype(bf16)


def updated(ids, got, table, accum):
    owned, width = table.shape
    tile = 512
    at = lambda i: (i, 0)
    return pl.pallas_call(
        functools.partial(update_kernel, tile),
        grid=(owned // tile,),
        in_specs=[
            pl.BlockSpec(ids.shape, lambda i: (0, 0)),
            pl.BlockSpec(got.shape, lambda i: (0, 0)),
            pl.BlockSpec((tile, width), at),
            pl.BlockSpec((tile, width), at),
        ],
        out_specs=[pl.BlockSpec((tile, width), at)] * 2,
        out_shape=[
            jax.ShapeDtypeStruct(table.shape, bf16),
            jax.ShapeDtypeStruct(accum.shape, f32),
        ],
        compiler_params=params(),
        cost_estimate=cost(2 * owned * got.shape[0] * width, 12 * owned * width),
        name="update",
    )(ids, got, table, accum)


def entering(end, log):
    size = lax.axis_size("tm")
    rows, width = end.shape
    parts = jnp.concatenate(
        [
            end.reshape(size, rows // size, width),
            jnp.broadcast_to(log[None], (size, 1, width)),
        ],
        axis=1,
    )
    parts = lax.all_to_all(parts, "tm", split_axis=0, concat_axis=0, tiled=True)
    ends, fades = parts[:, :-1], jnp.exp(parts[:, -1:])
    state = jnp.zeros((rows // size, width), f32)
    into = [state]
    for k in range(size - 1, 0, -1):
        state = ends[k] + fades[k] * state
        into.append(state)
    into = jnp.stack(into[::-1])
    into = lax.all_to_all(into, "tm", split_axis=0, concat_axis=0, tiled=True)
    return into.reshape(rows, width)


def on_device(out_grad, bc_proj, decay_log, skip_gain, owner, item_row, table, accum):
    users, events, width = out_grad.shape
    grad = out_grad.reshape(events, width)
    bc = bc_proj.reshape(events, 2 * STATE)
    decay = decay_log.reshape(HEADS, events)
    holders = lax.axis_size("tm") * lax.axis_size("table")
    capacity = 2 * events // holders

    carried, after, end, log = state_of(grad, bc, decay)
    place, ids = slots(
        owner.reshape(events // GROUP, GROUP), item_row.reshape(events // GROUP, GROUP),
        holders, capacity,
    )
    state = entering(end, log)
    got_ids = lax.all_to_all(ids, BOTH, split_axis=0, concat_axis=0, tiled=True)
    local, fade = local_rows(grad, bc, decay, skip_gain.reshape(1, HEADS), carried, after)
    rows = sent_rows(place, bc, local, fade, state, holders * capacity)
    got = lax.all_to_all(
        rows.reshape(holders, capacity, width), BOTH, split_axis=0, concat_axis=0, tiled=True
    ).reshape(holders * capacity, width)
    return updated(got_ids.reshape(-1, GROUP), got, table, accum)


def solution(mesh):
    placed = (
        P("table", "tm", None),
        P("table", "tm", None),
        P("table", None, "tm"),
        P(),
        P("table", "tm", None),
        P("table", "tm"),
        P(("tm", "table"), None),
        P(("tm", "table"), None),
    )
    return jax.shard_map(
        on_device,
        mesh=mesh,
        in_specs=placed,
        out_specs=(P(("tm", "table"), None), P(("tm", "table"), None)),
        check_vma=False,
    )
```

```python
import functools

import jax
import jax.numpy as jnp
from jax import lax
from jax.experimental import pallas as pl
from jax.experimental.pallas import tpu as pltpu
from jax.sharding import PartitionSpec as P

HEADS = 8
STATE = 64
GROUP = 256
ALIGN = 16
BOTH = ("tm", "table")
VMEM_BYTES = 60 * 1024 * 1024

learn_rate = 1.0

f32 = jnp.float32
bf16 = jnp.bfloat16


def params():
    return pltpu.CompilerParams(vmem_limit_bytes=VMEM_BYTES)


def cost(flops, moved, exps=0):
    return pl.CostEstimate(flops=flops, bytes_accessed=moved, transcendentals=exps)


def spread(columns, width):
    rows = columns.shape[0]
    head_dim = width // HEADS
    low = lax.broadcasted_iota(jnp.int32, (rows, 2 * head_dim), 1) < head_dim
    parts = [
        jnp.where(low, columns[:, h : h + 1], columns[:, h + 1 : h + 2]) for h in range(0, HEADS, 2)
    ]
    return jnp.concatenate(parts, axis=1)


def cumul_rows(decay):
    shape = (GROUP, GROUP)
    upto = lax.broadcasted_iota(jnp.int32, shape, 0) <= lax.broadcasted_iota(jnp.int32, shape, 1)
    upto = jnp.where(upto, 1.0, 0.0).astype(bf16)
    high = decay.astype(bf16)
    rest = decay - high.astype(f32)
    middle = rest.astype(bf16)
    low = (rest - middle.astype(f32)).astype(bf16)
    return (
        jnp.dot(low, upto, preferred_element_type=f32)
        + jnp.dot(middle, upto, preferred_element_type=f32)
        + jnp.dot(high, upto, preferred_element_type=f32)
    )


def two_parts(x):
    high = x.astype(bf16)
    return high, (x - high.astype(f32)).astype(bf16)


def pair_weights(grad):
    low = lax.broadcasted_iota(jnp.int32, grad.shape, 1) < grad.shape[1] // 2
    none = jnp.zeros_like(grad)
    return jnp.concatenate([jnp.where(low, grad, none), jnp.where(low, none, grad)], axis=0)


def state_kernel(
    grad_ref, bc_ref, decay_ref, carried_ref, after_ref, cumul_ref, end_ref
):
    events, width = grad_ref.shape
    blocks = events // GROUP
    two = 2 * width // HEADS
    cumul = cumul_rows(
        jnp.concatenate([decay_ref[:, b * GROUP : (b + 1) * GROUP] for b in range(blocks)], axis=0)
    )
    cumul_ref[...] = cumul
    grown = jnp.exp(cumul)
    low = lax.broadcasted_iota(jnp.int32, (1, two), 1) < two // 2
    state = jnp.zeros((STATE, width), f32)
    log = jnp.zeros((1, width), f32)
    for b in range(blocks - 1, -1, -1):
        at = pl.ds(b * GROUP, GROUP)
        c = jnp.transpose(bc_ref[at, :].astype(f32))[STATE:, :]
        ends, log_end = [], []
        for h in range(0, HEADS, 2):
            high, rest = [], []
            for k in (b * HEADS + h, b * HEADS + h + 1):
                one, other = two_parts(c * grown[k : k + 1, :])
                high.append(one)
                rest.append(other)
            scaled = jnp.concatenate(
                [jnp.concatenate(high, axis=1), jnp.concatenate(rest, axis=1)], axis=0
            )
            grad = grad_ref[at, h // 2 * two : (h // 2 + 1) * two]
            both = jnp.dot(scaled, pair_weights(grad), preferred_element_type=f32)
            ends.append(both[:STATE, :] + both[STATE:, :])
            last = cumul[b * HEADS + h : b * HEADS + h + 2, GROUP - 1 :]
            log_end.append(jnp.where(low, last[:1, :], last[1:, :]))
        carried_ref[b] = state
        after_ref[b] = log
        log_end = jnp.concatenate(log_end, axis=1)
        state = jnp.concatenate(ends, axis=1) + jnp.exp(log_end) * state
        log = log + log_end
    end_ref[:STATE, :] = state
    end_ref[STATE:, :] = jnp.broadcast_to(log, (8, width))


def state_of(grad, bc, decay):
    events, width = grad.shape
    blocks = events // GROUP
    return pl.pallas_call(
        state_kernel,
        out_shape=[
            jax.ShapeDtypeStruct((blocks, STATE, width), f32),
            jax.ShapeDtypeStruct((blocks, 1, width), f32),
            jax.ShapeDtypeStruct((blocks * HEADS, GROUP), f32),
            jax.ShapeDtypeStruct((STATE + 8, width), f32),
        ],
        compiler_params=params(),
        cost_estimate=cost(4 * events * width * STATE, 4 * events * width),
        name="state",
    )(grad, bc, decay)


def local_kernel(
    grad_ref, bc_ref, cumul_ref, skip_ref, carried_ref, after_ref, _, out_ref, fade_ref
):
    width = grad_ref.shape[1]
    two = 2 * width // HEADS
    half = GROUP // 2
    shape = (half, half)
    later = lax.broadcasted_iota(jnp.int32, shape, 1) >= lax.broadcasted_iota(jnp.int32, shape, 0)
    low = lax.broadcasted_iota(jnp.int32, (GROUP, two), 1) < two // 2
    rows = cumul_ref[...]
    columns = jnp.transpose(rows)
    for block in range(grad_ref.shape[0] // GROUP):
        at = pl.ds(block * GROUP, GROUP)
        past = jnp.exp(after_ref[block])
        b, c = bc_ref[at, :STATE], bc_ref[at, STATE:]
        scores = lax.dot_general(b, c, (((1,), (1,)), ((), ())), preferred_element_type=f32)
        first = jnp.where(later, scores[:half, :half], 0.0)
        across = scores[:half, half:]
        last = jnp.where(later, scores[half:, half:], 0.0)
        high, rest = two_parts(carried_ref[block])
        carried = jnp.dot(b, high, preferred_element_type=f32) + jnp.dot(
            b, rest, preferred_element_type=f32
        )
        for h in range(0, HEADS, 2):
            span = slice(h // 2 * two, (h // 2 + 1) * two)
            grad = grad_ref[at, span]
            weights = pair_weights(grad)
            upper, lower, wide, ends = [], [], [], []
            for k in (block * HEADS + h, block * HEADS + h + 1):
                row = rows[k : k + 1, :]
                column = jnp.broadcast_to(columns[:, k : k + 1], (GROUP, two))
                near = jnp.exp(jnp.minimum(row[:, :half] - column[:half, :], 0.0)) * first
                far = jnp.exp(row[:, half:] - column[:half, :]) * across
                end = jnp.exp(jnp.minimum(row[:, half:] - column[half:, :], 0.0)) * last
                upper += [near.astype(bf16), far.astype(bf16)]
                lower.append(end.astype(bf16))
                wide.append(row[:, GROUP - 1 :] - column)
            inner = jnp.concatenate(
                [
                    jnp.dot(
                        jnp.concatenate(upper, axis=1), weights, preferred_element_type=f32
                    ),
                    jnp.dot(
                        jnp.concatenate(lower, axis=1),
                        jnp.concatenate([weights[half:GROUP], weights[GROUP + half :]], axis=0),
                        preferred_element_type=f32,
                    ),
                ],
                axis=0,
            )
            fading = jnp.exp(jnp.where(low, wide[0], wide[1]))
            gain = jnp.where(low[:1, :], skip_ref[:, h : h + 1], skip_ref[:, h + 1 : h + 2])
            out_ref[at, span] = inner + carried[:, span] * fading + gain * grad.astype(f32)
            fade_ref[at, span] = fading * past[:, span]


def local_rows(grad, bc, cumul, skip, carried, after, earlier):
    events, width = grad.shape
    blocks = events // GROUP
    at = lambda i: (i, 0)
    step = 2
    return pl.pallas_call(
        local_kernel,
        grid=(blocks // step,),
        in_specs=[
            pl.BlockSpec((step * GROUP, width), at),
            pl.BlockSpec((step * GROUP, 2 * STATE), at),
            pl.BlockSpec((step * HEADS, GROUP), at),
            pl.BlockSpec((1, HEADS), lambda i: (0, 0)),
            pl.BlockSpec((step, STATE, width), lambda i: (i, 0, 0)),
            pl.BlockSpec((step, 1, width), lambda i: (i, 0, 0)),
            pl.BlockSpec(memory_space=pl.ANY),
        ],
        out_specs=[
            pl.BlockSpec((step * GROUP, width), at), pl.BlockSpec((step * GROUP, width), at)
        ],
        out_shape=[
            jax.ShapeDtypeStruct((events, width), f32),
            jax.ShapeDtypeStruct((events, width), f32),
        ],
        compiler_params=params(),
        cost_estimate=cost(
            blocks * GROUP * GROUP * (2 * width + 8 * HEADS), 10 * events * width,
            blocks * GROUP * GROUP * HEADS,
        ),
        name="local",
    )(grad, bc, cumul, skip, carried, after, earlier)


def slots_kernel(owner_ref, row_ref, place_ref, starts_ref, ids_ref):
    holders, _, capacity = ids_ref.shape
    spans = [slice(k * GROUP, (k + 1) * GROUP) for k in range(owner_ref.shape[1] // GROUP)]
    shape = (GROUP, GROUP)
    before = lax.broadcasted_iota(jnp.int32, shape, 0) < lax.broadcasted_iota(jnp.int32, shape, 1)
    before = jnp.where(before, 1.0, 0.0).astype(bf16)
    ones = jnp.ones((8, GROUP), bf16)
    count = jnp.zeros((holders, 1), f32)
    count_row = jnp.zeros((8, holders), f32)
    names = lax.broadcasted_iota(jnp.int32, (holders, GROUP), 0)
    ranks = lax.broadcasted_iota(jnp.int32, (capacity, GROUP), 0)
    high = jnp.zeros((holders, capacity), f32)
    low = jnp.zeros((holders, capacity), f32)
    across = (((1,), (1,)), ((), ()))
    hits_of, rank_of = [], []
    for at in spans:
        hits = jnp.where(names == owner_ref[:, at], 1.0, 0.0)
        hit = hits.astype(bf16)
        earlier = jnp.dot(hit, before, preferred_element_type=f32) + count
        rank = jnp.sum(hits * earlier, axis=0, keepdims=True)
        count = count + jnp.sum(hits, axis=1, keepdims=True)
        count_row = count_row + lax.dot_general(ones, hit, across, preferred_element_type=f32)
        hits_of.append(hits)
        rank_of.append(rank)
        ranked = jnp.where(ranks == rank.astype(jnp.int32), 1.0, 0.0).astype(bf16)
        named = row_ref[:, at] + 1
        upper = (hits * (named // 64).astype(f32)).astype(bf16)
        lower = (hits * (named % 64).astype(f32)).astype(bf16)
        high = high + lax.dot_general(upper, ranked, across, preferred_element_type=f32)
        low = low + lax.dot_general(lower, ranked, across, preferred_element_type=f32)
    ids_ref[:, 0, :] = (high * 64.0 + low).astype(jnp.int32)

    whole = lambda n: jnp.floor((n + (ALIGN - 1)) * (1.0 / ALIGN))
    square = (holders, holders)
    one = lax.broadcasted_iota(jnp.int32, square, 0)
    two = lax.broadcasted_iota(jnp.int32, square, 1)
    column = jnp.broadcast_to(whole(count), (holders, 128)).astype(bf16)
    sooner = jnp.where(two < one, 1.0, 0.0).astype(bf16)
    base = jnp.dot(sooner, column, preferred_element_type=f32)[:, :1] * ALIGN
    sooner = jnp.where(one < two, 1.0, 0.0).astype(bf16)
    starts = jnp.dot(whole(count_row).astype(bf16), sooner, preferred_element_type=f32) * ALIGN
    starts_ref[...] = starts[:1, :].astype(jnp.int32)
    for at, hits, rank in zip(spans, hits_of, rank_of):
        place = jnp.sum(hits * base, axis=0, keepdims=True) + rank
        place_ref[:, at] = place.astype(jnp.int32)


def slots(owner, row, holders, capacity):
    return pl.pallas_call(
        slots_kernel,
        out_shape=[
            jax.ShapeDtypeStruct(owner.shape, jnp.int32),
            jax.ShapeDtypeStruct((1, holders), jnp.int32),
            jax.ShapeDtypeStruct((holders, 1, capacity), jnp.int32),
        ],
        compiler_params=params(),
        cost_estimate=cost(2 * holders * owner.size * (GROUP + 2 * capacity), 8 * owner.size),
        name="slots",
    )(owner, row)


def send_kernel(
    blocks, tiles, sides_ref, starts_ref, place_ref, bc_ref, local_ref, fade_ref, end_ref, *refs,
):
    hops, (_, out_ref, high, low, rows, ordered, done) = refs[:-7], refs[-7:]
    step = pl.program_id(0)
    events, width = rows.shape
    block = events // blocks
    holders = starts_ref.shape[1]
    capacity = out_ref.shape[0] // holders
    tile = (ordered.shape[0] - capacity) // tiles

    @pl.when(step == 0)
    def _():
        state = jnp.zeros((STATE, width), f32)
        for hop in hops[::-1]:
            state = hop[:STATE, :] + jnp.exp(hop[STATE : STATE + 1, :]) * state
        through = end_ref[:STATE, :] + jnp.exp(end_ref[STATE : STATE + 1, :]) * state
        high[...], low[...] = two_parts(jnp.where(sides_ref[0] == 0, through, state))
        ordered[tiles * tile :, :] = jnp.zeros((capacity, width), bf16)

    @pl.when(step < blocks)
    def _():
        b = bc_ref[:, :STATE]
        part = jnp.dot(b, high[...], preferred_element_type=f32) + jnp.dot(
            b, low[...], preferred_element_type=f32
        )
        row = (local_ref[...] + part * fade_ref[...]).astype(bf16)
        rows[pl.ds(pl.multiple_of(step * block, block), block), :] = row

    @pl.when(step >= blocks)
    def _():
        first = pl.multiple_of((step - blocks) * tile, tile)
        names = lax.broadcasted_iota(jnp.int32, (tile, events), 0) + first
        chosen = jnp.where(names == place_ref[...], 1.0, 0.0).astype(bf16)
        ordered[pl.ds(first, tile), :] = jnp.dot(
            chosen, rows[...], preferred_element_type=f32
        ).astype(bf16)

    @pl.when(step == blocks + tiles - 1)
    def _():
        def copy(k):
            start = pl.multiple_of(starts_ref[0, k], ALIGN)
            return pltpu.make_async_copy(
                ordered.at[pl.ds(start, capacity), :],
                out_ref.at[pl.ds(k * capacity, capacity), :],
                done.at[k],
            )

        for k in range(holders):
            copy(k).start()
        for k in range(holders):
            copy(k).wait()


def sent_rows(sides, starts, place, bc, local, fade, partner, hops, capacity, earlier):
    events, width = local.shape
    holders = starts.shape[1]
    blocks, tiles = 4, 4
    block = events // blocks
    ordered = -(-(events + (ALIGN - 1) * holders) // (tiles * ALIGN)) * tiles * ALIGN
    whole = lambda a: pl.BlockSpec(a.shape, lambda i: (0,) * a.ndim)
    at = lambda i: (jnp.minimum(i, blocks - 1), 0)
    smem = pl.BlockSpec(memory_space=pltpu.SMEM)
    return pl.pallas_call(
        functools.partial(send_kernel, blocks, tiles),
        grid=(blocks + tiles,),
        in_specs=[
            smem,
            smem,
            whole(place),
            pl.BlockSpec((block, 2 * STATE), at),
            pl.BlockSpec((block, width), at),
            pl.BlockSpec((block, width), at),
            whole(partner),
        ]
        + [whole(hop) for hop in hops]
        + [pl.BlockSpec(memory_space=pl.ANY)],
        out_specs=pl.BlockSpec(memory_space=pl.ANY),
        out_shape=jax.ShapeDtypeStruct((holders * capacity, width), bf16),
        scratch_shapes=[
            pltpu.VMEM((STATE, width), bf16),
            pltpu.VMEM((STATE, width), bf16),
            pltpu.VMEM((events, width), bf16),
            pltpu.VMEM((ordered + capacity, width), bf16),
            pltpu.SemaphoreType.DMA((holders,)),
        ],
        compiler_params=params(),
        cost_estimate=cost(2 * ordered * events * width, 12 * events * width),
        name="send",
    )(sides, starts, place, bc, local, fade, partner, *hops, earlier)


def update_kernel(tile, ids_ref, got_ref, table_ref, accum_ref, new_table_ref, new_accum_ref):
    parts, lanes = ids_ref.shape
    ids = jnp.concatenate([ids_ref[k : k + 1, :] for k in range(parts)], axis=1)
    names = lax.broadcasted_iota(jnp.int32, (tile, parts * lanes), 0)
    names = names + (pl.program_id(0) * tile + 1)
    chosen = jnp.where(names == ids, 1.0, 0.0).astype(bf16)
    total = jnp.dot(chosen, got_ref[...], preferred_element_type=f32)
    accum = accum_ref[...] + total * total
    new_accum_ref[...] = accum
    new_table_ref[...] = (
        table_ref[...].astype(f32) - learn_rate * total * lax.rsqrt(accum)
    ).astype(bf16)


def updated(ids, got, table, accum):
    owned, width = table.shape
    tile = 512
    block = pl.BlockSpec((tile, width), lambda i: (i, 0))
    whole = lambda a: pl.BlockSpec(a.shape, lambda i: (0, 0))
    return pl.pallas_call(
        functools.partial(update_kernel, tile),
        grid=(owned // tile,),
        in_specs=[whole(ids), whole(got), block, block],
        out_specs=[block] * 2,
        out_shape=[
            jax.ShapeDtypeStruct(table.shape, bf16),
            jax.ShapeDtypeStruct(accum.shape, f32),
        ],
        compiler_params=params(),
        cost_estimate=cost(2 * owned * got.shape[0] * width, 12 * owned * width),
        name="update",
    )(ids, got, table, accum)


def pair_kernel(sides_ref, end_ref, partner_ref, _, pair_ref):
    first = sides_ref[0] == 0
    end, partner = end_ref[...], partner_ref[...]
    early = jnp.where(first, end, partner)
    late = jnp.where(first, partner, end)
    fade = jnp.exp(early[STATE : STATE + 1, :])
    pair_ref[:STATE, :] = early[:STATE, :] + fade * late[:STATE, :]
    pair_ref[STATE:, :] = early[STATE:, :] + late[STATE:, :]


def pair_state(sides, end, partner, earlier):
    vmem = pl.BlockSpec(memory_space=pltpu.VMEM)
    return pl.pallas_call(
        pair_kernel,
        in_specs=[
            pl.BlockSpec(memory_space=pltpu.SMEM), vmem, vmem, pl.BlockSpec(memory_space=pl.ANY)
        ],
        out_shape=jax.ShapeDtypeStruct(end.shape, f32),
        compiler_params=params(),
        cost_estimate=cost(4 * end.size, 12 * end.size),
        name="pair",
    )(sides, end, partner, earlier)


def on_device(out_grad, bc_proj, decay_log, skip_gain, owner, item_row, table, accum):
    users, events, width = out_grad.shape
    grad = out_grad.reshape(events, width)
    bc = bc_proj.reshape(events, 2 * STATE)
    decay = decay_log.reshape(HEADS, events)
    size = lax.axis_size("tm")
    holders = size * lax.axis_size("table")
    capacity = 2 * events // holders
    side = lax.axis_index("tm") % 2
    sides = jnp.broadcast_to(side, (1,)).astype(jnp.int32)

    place, starts, ids = slots(owner.reshape(1, events), item_row, holders, capacity)
    got_ids = lax.all_to_all(ids, BOTH, split_axis=0, concat_axis=0, tiled=True)
    carried, after, cumul, end = state_of(grad, bc, decay)
    partner = lax.ppermute(end, "tm", [(i, i ^ 1) for i in range(size)])
    pair = pair_state(sides, end, partner, place)
    hops = [
        lax.ppermute(pair, "tm", [(i, i - k) for i in range(k, size)]) for k in range(2, size, 2)
    ]
    local, fade = local_rows(
        grad, bc, cumul, skip_gain.reshape(1, HEADS), carried, after, pair
    )
    rows = sent_rows(
        sides, starts, place, bc, local, fade, partner, hops, capacity, got_ids
    )
    got = lax.all_to_all(
        rows.reshape(holders, capacity, width), BOTH, split_axis=0, concat_axis=0, tiled=True
    ).reshape(holders * capacity, width)
    return updated(got_ids.reshape(-1, 128), got, table, accum)


def solution(mesh):
    placed = (
        P("table", "tm", None),
        P("table", "tm", None),
        P("table", None, "tm"),
        P(),
        P("table", "tm", None),
        P("table", "tm"),
        P(("tm", "table"), None),
        P(("tm", "table"), None),
    )
    return jax.shard_map(
        on_device,
        mesh=mesh,
        in_specs=placed,
        out_specs=(P(("tm", "table"), None), P(("tm", "table"), None)),
        check_vma=False,
    )
```

```python
import functools

import jax
import jax.numpy as jnp
from jax import lax
from jax.experimental import pallas as pl
from jax.experimental.pallas import tpu as pltpu
from jax.sharding import PartitionSpec as P

HEADS = 8
STATE = 64
GROUP = 256
ALIGN = 16
PARTS = 2
PART_HEADS = HEADS // PARTS
BOTH = ("tm", "table")
VMEM_BYTES = 60 * 1024 * 1024

learn_rate = 1.0

f32 = jnp.float32
bf16 = jnp.bfloat16


def params():
    return pltpu.CompilerParams(vmem_limit_bytes=VMEM_BYTES)


def cost(flops, moved, exps=0):
    return pl.CostEstimate(flops=flops, bytes_accessed=moved, transcendentals=exps)


def cumul_rows(decay):
    shape = (GROUP, GROUP)
    upto = lax.broadcasted_iota(jnp.int32, shape, 0) <= lax.broadcasted_iota(jnp.int32, shape, 1)
    upto = jnp.where(upto, 1.0, 0.0).astype(bf16)
    high = decay.astype(bf16)
    rest = decay - high.astype(f32)
    middle = rest.astype(bf16)
    low = (rest - middle.astype(f32)).astype(bf16)
    return (
        jnp.dot(low, upto, preferred_element_type=f32)
        + jnp.dot(middle, upto, preferred_element_type=f32)
        + jnp.dot(high, upto, preferred_element_type=f32)
    )


def two_parts(x):
    high = x.astype(bf16)
    return high, (x - high.astype(f32)).astype(bf16)


def pair_weights(grad):
    low = lax.broadcasted_iota(jnp.int32, grad.shape, 1) < grad.shape[1] // 2
    none = jnp.zeros_like(grad)
    return jnp.concatenate([jnp.where(low, grad, none), jnp.where(low, none, grad)], axis=0)


def state_kernel(
    grad_ref, bc_ref, decay_ref, carried_ref, after_ref, cumul_ref, end_ref
):
    events, width = grad_ref.shape
    blocks = events // GROUP
    two = 2 * width // HEADS
    cumul = cumul_rows(
        jnp.concatenate([decay_ref[:, b * GROUP : (b + 1) * GROUP] for b in range(blocks)], axis=0)
    )
    cumul_ref[...] = cumul
    grown = jnp.exp(cumul)
    low = lax.broadcasted_iota(jnp.int32, (1, two), 1) < two // 2
    state = jnp.zeros((STATE, width), f32)
    log = jnp.zeros((1, width), f32)
    for b in range(blocks - 1, -1, -1):
        at = pl.ds(b * GROUP, GROUP)
        c = jnp.transpose(bc_ref[at, :].astype(f32))[STATE:, :]
        ends, log_end = [], []
        for h in range(0, HEADS, 2):
            high, rest = [], []
            for k in (b * HEADS + h, b * HEADS + h + 1):
                one, other = two_parts(c * grown[k : k + 1, :])
                high.append(one)
                rest.append(other)
            scaled = jnp.concatenate(
                [jnp.concatenate(high, axis=1), jnp.concatenate(rest, axis=1)], axis=0
            )
            grad = grad_ref[at, h // 2 * two : (h // 2 + 1) * two]
            both = jnp.dot(scaled, pair_weights(grad), preferred_element_type=f32)
            ends.append(both[:STATE, :] + both[STATE:, :])
            last = cumul[b * HEADS + h : b * HEADS + h + 2, GROUP - 1 :]
            log_end.append(jnp.where(low, last[:1, :], last[1:, :]))
        carried_ref[b] = state
        after_ref[b] = log
        log_end = jnp.concatenate(log_end, axis=1)
        state = jnp.concatenate(ends, axis=1) + jnp.exp(log_end) * state
        log = log + log_end
    end_ref[:STATE, :] = state
    end_ref[STATE:, :] = jnp.broadcast_to(log, (8, width))


def state_of(grad, bc, decay):
    events, width = grad.shape
    blocks = events // GROUP
    return pl.pallas_call(
        state_kernel,
        out_shape=[
            jax.ShapeDtypeStruct((blocks, STATE, width), f32),
            jax.ShapeDtypeStruct((blocks, 1, width), f32),
            jax.ShapeDtypeStruct((blocks * HEADS, GROUP), f32),
            jax.ShapeDtypeStruct((STATE + 8, width), f32),
        ],
        compiler_params=params(),
        cost_estimate=cost(4 * events * width * STATE, 4 * events * width),
        name="state",
    )(grad, bc, decay)


def local_kernel(
    part, grad_ref, bc_ref, cumul_ref, skip_ref, carried_ref, after_ref, _, out_ref, fade_ref
):
    width = grad_ref.shape[1]
    two = 2 * width // PART_HEADS
    half = GROUP // 2
    shape = (half, half)
    later = lax.broadcasted_iota(jnp.int32, shape, 1) >= lax.broadcasted_iota(jnp.int32, shape, 0)
    low = lax.broadcasted_iota(jnp.int32, (GROUP, two), 1) < two // 2
    rows = cumul_ref[...]
    columns = jnp.transpose(rows)
    for block in range(grad_ref.shape[0] // GROUP):
        at = pl.ds(block * GROUP, GROUP)
        past = jnp.exp(after_ref[block])
        b, c = bc_ref[at, :STATE], bc_ref[at, STATE:]
        scores = lax.dot_general(b, c, (((1,), (1,)), ((), ())), preferred_element_type=f32)
        first = jnp.where(later, scores[:half, :half], 0.0)
        across = scores[:half, half:]
        last = jnp.where(later, scores[half:, half:], 0.0)
        high, rest = two_parts(carried_ref[block])
        carried = jnp.dot(b, high, preferred_element_type=f32) + jnp.dot(
            b, rest, preferred_element_type=f32
        )
        for h in range(0, PART_HEADS, 2):
            head = part * PART_HEADS + h
            span = slice(h // 2 * two, (h // 2 + 1) * two)
            grad = grad_ref[at, span]
            weights = pair_weights(grad)
            upper, lower, wide, ends = [], [], [], []
            for k in (block * HEADS + head, block * HEADS + head + 1):
                row = rows[k : k + 1, :]
                column = jnp.broadcast_to(columns[:, k : k + 1], (GROUP, two))
                near = jnp.exp(jnp.minimum(row[:, :half] - column[:half, :], 0.0)) * first
                far = jnp.exp(row[:, half:] - column[:half, :]) * across
                end = jnp.exp(jnp.minimum(row[:, half:] - column[half:, :], 0.0)) * last
                upper += [near.astype(bf16), far.astype(bf16)]
                lower.append(end.astype(bf16))
                wide.append(row[:, GROUP - 1 :] - column)
            inner = jnp.concatenate(
                [
                    jnp.dot(
                        jnp.concatenate(upper, axis=1), weights, preferred_element_type=f32
                    ),
                    jnp.dot(
                        jnp.concatenate(lower, axis=1),
                        jnp.concatenate([weights[half:GROUP], weights[GROUP + half :]], axis=0),
                        preferred_element_type=f32,
                    ),
                ],
                axis=0,
            )
            fading = jnp.exp(jnp.where(low, wide[0], wide[1]))
            gain = jnp.where(low[:1, :], skip_ref[:, head : head + 1], skip_ref[:, head + 1 : head + 2])
            out_ref[at, span] = inner + carried[:, span] * fading + gain * grad.astype(f32)
            fade_ref[at, span] = fading * past[:, span]


def local_rows(part, grad, bc, cumul, skip, carried, after, earlier):
    events = grad.shape[0]
    width = grad.shape[1] // PARTS
    blocks = events // GROUP
    at = lambda i: (i, 0)
    step = 4
    return pl.pallas_call(
        functools.partial(local_kernel, part),
        grid=(blocks // step,),
        in_specs=[
            pl.BlockSpec((step * GROUP, width), lambda i: (i, part)),
            pl.BlockSpec((step * GROUP, 2 * STATE), at),
            pl.BlockSpec((step * HEADS, GROUP), at),
            pl.BlockSpec((1, HEADS), lambda i: (0, 0)),
            pl.BlockSpec((step, STATE, width), lambda i: (i, 0, part)),
            pl.BlockSpec((step, 1, width), lambda i: (i, 0, part)),
            pl.BlockSpec(memory_space=pl.ANY),
        ],
        out_specs=[
            pl.BlockSpec((step * GROUP, width), at), pl.BlockSpec((step * GROUP, width), at)
        ],
        out_shape=[
            jax.ShapeDtypeStruct((events, width), f32),
            jax.ShapeDtypeStruct((events, width), f32),
        ],
        compiler_params=params(),
        cost_estimate=cost(
            blocks * GROUP * GROUP * (2 * width + 8 * HEADS), 10 * events * width,
            blocks * GROUP * GROUP * HEADS,
        ),
        name="local",
    )(grad, bc, cumul, skip, carried, after, earlier)


def slots_kernel(owner_ref, row_ref, place_ref, starts_ref, ids_ref):
    holders, _, capacity = ids_ref.shape
    spans = [slice(k * GROUP, (k + 1) * GROUP) for k in range(owner_ref.shape[1] // GROUP)]
    shape = (GROUP, GROUP)
    before = lax.broadcasted_iota(jnp.int32, shape, 0) < lax.broadcasted_iota(jnp.int32, shape, 1)
    before = jnp.where(before, 1.0, 0.0).astype(bf16)
    ones = jnp.ones((8, GROUP), bf16)
    count = jnp.zeros((holders, 1), f32)
    count_row = jnp.zeros((8, holders), f32)
    names = lax.broadcasted_iota(jnp.int32, (holders, GROUP), 0)
    ranks = lax.broadcasted_iota(jnp.int32, (capacity, GROUP), 0)
    high = jnp.zeros((holders, capacity), f32)
    low = jnp.zeros((holders, capacity), f32)
    across = (((1,), (1,)), ((), ()))
    hits_of, rank_of = [], []
    for at in spans:
        hits = jnp.where(names == owner_ref[:, at], 1.0, 0.0)
        hit = hits.astype(bf16)
        earlier = jnp.dot(hit, before, preferred_element_type=f32) + count
        rank = jnp.sum(hits * earlier, axis=0, keepdims=True)
        count = count + jnp.sum(hits, axis=1, keepdims=True)
        count_row = count_row + lax.dot_general(ones, hit, across, preferred_element_type=f32)
        hits_of.append(hits)
        rank_of.append(rank)
        ranked = jnp.where(ranks == rank.astype(jnp.int32), 1.0, 0.0).astype(bf16)
        named = row_ref[:, at] + 1
        upper = (hits * (named // 64).astype(f32)).astype(bf16)
        lower = (hits * (named % 64).astype(f32)).astype(bf16)
        high = high + lax.dot_general(upper, ranked, across, preferred_element_type=f32)
        low = low + lax.dot_general(lower, ranked, across, preferred_element_type=f32)
    ids_ref[:, 0, :] = (high * 64.0 + low).astype(jnp.int32)

    whole = lambda n: jnp.floor((n + (ALIGN - 1)) * (1.0 / ALIGN))
    square = (holders, holders)
    one = lax.broadcasted_iota(jnp.int32, square, 0)
    two = lax.broadcasted_iota(jnp.int32, square, 1)
    column = jnp.broadcast_to(whole(count), (holders, 128)).astype(bf16)
    sooner = jnp.where(two < one, 1.0, 0.0).astype(bf16)
    base = jnp.dot(sooner, column, preferred_element_type=f32)[:, :1] * ALIGN
    sooner = jnp.where(one < two, 1.0, 0.0).astype(bf16)
    starts = jnp.dot(whole(count_row).astype(bf16), sooner, preferred_element_type=f32) * ALIGN
    starts_ref[...] = starts[:1, :].astype(jnp.int32)
    for at, hits, rank in zip(spans, hits_of, rank_of):
        place = jnp.sum(hits * base, axis=0, keepdims=True) + rank
        place_ref[:, at] = place.astype(jnp.int32)


def slots(owner, row, holders, capacity):
    return pl.pallas_call(
        slots_kernel,
        out_shape=[
            jax.ShapeDtypeStruct(owner.shape, jnp.int32),
            jax.ShapeDtypeStruct((1, holders), jnp.int32),
            jax.ShapeDtypeStruct((holders, 1, capacity), jnp.int32),
        ],
        compiler_params=params(),
        cost_estimate=cost(2 * holders * owner.size * (GROUP + 2 * capacity), 8 * owner.size),
        name="slots",
    )(owner, row)


def send_kernel(
    blocks, tiles, sides_ref, starts_ref, place_ref, bc_ref, local_ref, fade_ref, end_ref, *refs,
):
    hops, (_, out_ref, high, low, rows, ordered, done) = refs[:-7], refs[-7:]
    step = pl.program_id(0)
    events, width = rows.shape
    block = events // blocks
    holders = starts_ref.shape[1]
    capacity = out_ref.shape[0] // holders
    tile = (ordered.shape[0] - capacity) // tiles

    @pl.when(step == 0)
    def _():
        state = jnp.zeros((STATE, width), f32)
        for hop in hops[::-1]:
            state = hop[:STATE, :] + jnp.exp(hop[STATE : STATE + 1, :]) * state
        through = end_ref[:STATE, :] + jnp.exp(end_ref[STATE : STATE + 1, :]) * state
        high[...], low[...] = two_parts(jnp.where(sides_ref[0] == 0, through, state))
        ordered[tiles * tile :, :] = jnp.zeros((capacity, width), bf16)

    @pl.when(step < blocks)
    def _():
        b = bc_ref[:, :STATE]
        part = jnp.dot(b, high[...], preferred_element_type=f32) + jnp.dot(
            b, low[...], preferred_element_type=f32
        )
        row = (local_ref[...] + part * fade_ref[...]).astype(bf16)
        rows[pl.ds(pl.multiple_of(step * block, block), block), :] = row

    @pl.when(step >= blocks)
    def _():
        first = pl.multiple_of((step - blocks) * tile, tile)
        names = lax.broadcasted_iota(jnp.int32, (tile, events), 0) + first
        chosen = jnp.where(names == place_ref[...], 1.0, 0.0).astype(bf16)
        ordered[pl.ds(first, tile), :] = jnp.dot(
            chosen, rows[...], preferred_element_type=f32
        ).astype(bf16)

    @pl.when(step == blocks + tiles - 1)
    def _():
        def copy(k):
            start = pl.multiple_of(starts_ref[0, k], ALIGN)
            return pltpu.make_async_copy(
                ordered.at[pl.ds(start, capacity), :],
                out_ref.at[pl.ds(k * capacity, capacity), :],
                done.at[k],
            )

        for k in range(holders):
            copy(k).start()
        for k in range(holders):
            copy(k).wait()


def sent_rows(part, sides, starts, place, bc, local, fade, partner, hops, capacity, earlier):
    events, width = local.shape
    holders = starts.shape[1]
    blocks, tiles = 2, 1
    block = events // blocks
    ordered = -(-(events + (ALIGN - 1) * holders) // (tiles * ALIGN)) * tiles * ALIGN
    whole = lambda a: pl.BlockSpec(a.shape, lambda i: (0,) * a.ndim)
    at = lambda i: (jnp.minimum(i, blocks - 1), 0)
    smem = pl.BlockSpec(memory_space=pltpu.SMEM)
    return pl.pallas_call(
        functools.partial(send_kernel, blocks, tiles),
        grid=(blocks + tiles,),
        in_specs=[
            smem,
            smem,
            whole(place),
            pl.BlockSpec((block, 2 * STATE), at),
            pl.BlockSpec((block, width), at),
            pl.BlockSpec((block, width), at),
        ]
        + [pl.BlockSpec((hop.shape[0], width), lambda i: (0, part)) for hop in (partner, *hops)]
        + [pl.BlockSpec(memory_space=pl.ANY)],
        out_specs=pl.BlockSpec(memory_space=pltpu.HBM),
        out_shape=jax.ShapeDtypeStruct((holders * capacity, width), bf16),
        scratch_shapes=[
            pltpu.VMEM((STATE, width), bf16),
            pltpu.VMEM((STATE, width), bf16),
            pltpu.VMEM((events, width), bf16),
            pltpu.VMEM((ordered + capacity, width), bf16),
            pltpu.SemaphoreType.DMA((holders,)),
        ],
        compiler_params=params(),
        cost_estimate=cost(2 * ordered * events * width, 12 * events * width),
        name="send",
    )(sides, starts, place, bc, local, fade, partner, *hops, earlier)


def update_kernel(tile, ids_ref, got_ref, table_ref, accum_ref, *refs):
    new_table_ref, new_accum_ref = refs[-2:]
    parts, lanes = ids_ref.shape
    ids = jnp.concatenate([ids_ref[k : k + 1, :] for k in range(parts)], axis=1)
    names = lax.broadcasted_iota(jnp.int32, (tile, parts * lanes), 0)
    names = names + (pl.program_id(0) * tile + 1)
    chosen = jnp.where(names == ids, 1.0, 0.0).astype(bf16)
    total = jnp.dot(chosen, got_ref[...], preferred_element_type=f32)
    accum = accum_ref[...] + total * total
    new_accum_ref[...] = accum
    new_table_ref[...] = (
        table_ref[...].astype(f32) - learn_rate * total * lax.rsqrt(accum)
    ).astype(bf16)


def updated(part, ids, got, table, accum, before):
    owned = table.shape[0]
    width = got.shape[1]
    tile = 512
    block = pl.BlockSpec((tile, width), lambda i: (i, part))
    whole = lambda a: pl.BlockSpec(a.shape, lambda i: (0, 0))
    return pl.pallas_call(
        functools.partial(update_kernel, tile),
        grid=(owned // tile,),
        in_specs=[whole(ids), whole(got), block, block]
        + [pl.BlockSpec(memory_space=pl.ANY)] * len(before),
        out_specs=[block] * 2,
        out_shape=[
            jax.ShapeDtypeStruct(table.shape, bf16),
            jax.ShapeDtypeStruct(accum.shape, f32),
        ],
        input_output_aliases={4 + k: k for k in range(len(before))},
        compiler_params=params(),
        cost_estimate=cost(2 * owned * got.shape[0] * width, 12 * owned * width),
        name="update",
    )(ids, got, table, accum, *before)


def pair_state(side, end, partner):
    early = jnp.where(side == 0, end, partner)
    late = jnp.where(side == 0, partner, end)
    return jnp.concatenate(
        [
            early[:STATE] + jnp.exp(early[STATE : STATE + 1]) * late[:STATE],
            early[STATE:] + late[STATE:],
        ]
    )


def on_device(out_grad, bc_proj, decay_log, skip_gain, owner, item_row, table, accum):
    users, events, width = out_grad.shape
    grad = out_grad.reshape(events, width)
    bc = bc_proj.reshape(events, 2 * STATE)
    decay = decay_log.reshape(HEADS, events)
    size = lax.axis_size("tm")
    holders = size * lax.axis_size("table")
    capacity = 2 * events // holders
    side = lax.axis_index("tm") % 2
    sides = jnp.broadcast_to(side, (1,)).astype(jnp.int32)

    place, starts, ids = slots(owner.reshape(1, events), item_row, holders, capacity)
    got_ids = lax.all_to_all(ids, BOTH, split_axis=0, concat_axis=0, tiled=True)
    ids = got_ids.reshape(-1, 128)
    skip = skip_gain.reshape(1, HEADS)

    carried, after, cumul, end = state_of(grad, bc, decay)
    partner = lax.ppermute(end, "tm", [(i, i ^ 1) for i in range(size)])
    place, partner = lax.optimization_barrier((place, partner))
    pair = pair_state(side, end, partner)
    hops = [
        lax.ppermute(pair, "tm", [(i, i - k) for i in range(k, size)]) for k in range(2, size, 2)
    ]

    new, earlier = (), pair
    for part in range(PARTS):
        local, fade = local_rows(part, grad, bc, cumul, skip, carried, after, earlier)
        rows = sent_rows(
            part, sides, starts, place, bc, local, fade, partner, hops, capacity, got_ids
        )
        got = lax.all_to_all(
            rows.reshape(holders, capacity, -1), BOTH, split_axis=0, concat_axis=0, tiled=True
        )
        new = updated(part, ids, got.reshape(holders * capacity, -1), table, accum, new)
        earlier = rows
    return new


def solution(mesh):
    placed = (
        P("table", "tm", None),
        P("table", "tm", None),
        P("table", None, "tm"),
        P(),
        P("table", "tm", None),
        P("table", "tm"),
        P(("tm", "table"), None),
        P(("tm", "table"), None),
    )
    return jax.shard_map(
        on_device,
        mesh=mesh,
        in_specs=placed,
        out_specs=(P(("tm", "table"), None), P(("tm", "table"), None)),
        check_vma=False,
    )
```

```python
import functools

import jax
import jax.numpy as jnp
from jax import lax
from jax.experimental import pallas as pl
from jax.experimental.pallas import tpu as pltpu
from jax.sharding import PartitionSpec as P

HEADS = 8
STATE = 64
GROUP = 256
ALIGN = 16
PARTS = 2
PART_HEADS = HEADS // PARTS
BOTH = ("tm", "table")
MIB = 1024 * 1024

learn_rate = 1.0

f32 = jnp.float32
bf16 = jnp.bfloat16


def params(mib=60):
    return pltpu.CompilerParams(vmem_limit_bytes=mib * MIB)


def cost(flops, moved, exps=0):
    return pl.CostEstimate(flops=flops, bytes_accessed=moved, transcendentals=exps)


def cumul_rows(decay):
    shape = (GROUP, GROUP)
    upto = lax.broadcasted_iota(jnp.int32, shape, 0) <= lax.broadcasted_iota(jnp.int32, shape, 1)
    upto = jnp.where(upto, 1.0, 0.0).astype(bf16)
    high = decay.astype(bf16)
    rest = decay - high.astype(f32)
    middle = rest.astype(bf16)
    low = (rest - middle.astype(f32)).astype(bf16)
    return (
        jnp.dot(low, upto, preferred_element_type=f32)
        + jnp.dot(middle, upto, preferred_element_type=f32)
        + jnp.dot(high, upto, preferred_element_type=f32)
    )


def two_parts(x):
    high = x.astype(bf16)
    return high, (x - high.astype(f32)).astype(bf16)


def pair_weights(grad):
    low = lax.broadcasted_iota(jnp.int32, grad.shape, 1) < grad.shape[1] // 2
    none = jnp.zeros_like(grad)
    return jnp.concatenate([jnp.where(low, grad, none), jnp.where(low, none, grad)], axis=0)


def state_kernel(
    grad_ref, bc_ref, decay_ref, carried_ref, after_ref, cumul_ref, end_ref
):
    events, width = grad_ref.shape
    blocks = events // GROUP
    two = 2 * width // HEADS
    cumul = cumul_rows(
        jnp.concatenate([decay_ref[:, b * GROUP : (b + 1) * GROUP] for b in range(blocks)], axis=0)
    )
    cumul_ref[...] = cumul
    grown = jnp.exp(cumul)
    low = lax.broadcasted_iota(jnp.int32, (1, two), 1) < two // 2
    state = jnp.zeros((STATE, width), f32)
    log = jnp.zeros((1, width), f32)
    for b in range(blocks - 1, -1, -1):
        at = pl.ds(b * GROUP, GROUP)
        c = jnp.transpose(bc_ref[at, :].astype(f32))[STATE:, :]
        ends, log_end = [], []
        for h in range(0, HEADS, 2):
            high, rest = [], []
            for k in (b * HEADS + h, b * HEADS + h + 1):
                one, other = two_parts(c * grown[k : k + 1, :])
                high.append(one)
                rest.append(other)
            scaled = jnp.concatenate(
                [jnp.concatenate(high, axis=1), jnp.concatenate(rest, axis=1)], axis=0
            )
            grad = grad_ref[at, h // 2 * two : (h // 2 + 1) * two]
            both = jnp.dot(scaled, pair_weights(grad), preferred_element_type=f32)
            ends.append(both[:STATE, :] + both[STATE:, :])
            last = cumul[b * HEADS + h : b * HEADS + h + 2, GROUP - 1 :]
            log_end.append(jnp.where(low, last[:1, :], last[1:, :]))
        carried_ref[b] = state
        after_ref[b] = log
        log_end = jnp.concatenate(log_end, axis=1)
        state = jnp.concatenate(ends, axis=1) + jnp.exp(log_end) * state
        log = log + log_end
    end_ref[:STATE, :] = state
    end_ref[STATE:, :] = jnp.broadcast_to(log, (8, width))


def state_of(grad, bc, decay):
    events, width = grad.shape
    blocks = events // GROUP
    return pl.pallas_call(
        state_kernel,
        out_shape=[
            jax.ShapeDtypeStruct((blocks, STATE, width), f32),
            jax.ShapeDtypeStruct((blocks, 1, width), f32),
            jax.ShapeDtypeStruct((blocks * HEADS, GROUP), f32),
            jax.ShapeDtypeStruct((STATE + 8, width), f32),
        ],
        compiler_params=params(),
        cost_estimate=cost(4 * events * width * STATE, 4 * events * width),
        name="state",
    )(grad, bc, decay)


def local_kernel(
    part, grad_ref, bc_ref, cumul_ref, skip_ref, carried_ref, after_ref, _, out_ref, fade_ref
):
    width = grad_ref.shape[1]
    two = 2 * width // PART_HEADS
    half = GROUP // 2
    shape = (half, half)
    later = lax.broadcasted_iota(jnp.int32, shape, 1) >= lax.broadcasted_iota(jnp.int32, shape, 0)
    low = lax.broadcasted_iota(jnp.int32, (GROUP, two), 1) < two // 2
    rows = cumul_ref[...]
    columns = jnp.transpose(rows)
    for block in range(grad_ref.shape[0] // GROUP):
        at = pl.ds(block * GROUP, GROUP)
        past = jnp.exp(after_ref[block])
        b, c = bc_ref[at, :STATE], bc_ref[at, STATE:]
        scores = lax.dot_general(b, c, (((1,), (1,)), ((), ())), preferred_element_type=f32)
        first = jnp.where(later, scores[:half, :half], 0.0)
        across = scores[:half, half:]
        last = jnp.where(later, scores[half:, half:], 0.0)
        high, rest = two_parts(carried_ref[block])
        carried = jnp.dot(b, high, preferred_element_type=f32) + jnp.dot(
            b, rest, preferred_element_type=f32
        )
        for h in range(0, PART_HEADS, 2):
            head = part * PART_HEADS + h
            span = slice(h // 2 * two, (h // 2 + 1) * two)
            grad = grad_ref[at, span]
            weights = pair_weights(grad)
            upper, lower, wide, ends = [], [], [], []
            for k in (block * HEADS + head, block * HEADS + head + 1):
                row = rows[k : k + 1, :]
                column = jnp.broadcast_to(columns[:, k : k + 1], (GROUP, two))
                near = jnp.exp(jnp.minimum(row[:, :half] - column[:half, :], 0.0)) * first
                far = jnp.exp(row[:, half:] - column[:half, :]) * across
                end = jnp.exp(jnp.minimum(row[:, half:] - column[half:, :], 0.0)) * last
                upper += [near.astype(bf16), far.astype(bf16)]
                lower.append(end.astype(bf16))
                wide.append(row[:, GROUP - 1 :] - column)
            inner = jnp.concatenate(
                [
                    jnp.dot(
                        jnp.concatenate(upper, axis=1), weights, preferred_element_type=f32
                    ),
                    jnp.dot(
                        jnp.concatenate(lower, axis=1),
                        jnp.concatenate([weights[half:GROUP], weights[GROUP + half :]], axis=0),
                        preferred_element_type=f32,
                    ),
                ],
                axis=0,
            )
            fading = jnp.exp(jnp.where(low, wide[0], wide[1]))
            gain = jnp.where(low[:1, :], skip_ref[:, head : head + 1], skip_ref[:, head + 1 : head + 2])
            out_ref[at, span] = inner + carried[:, span] * fading + gain * grad.astype(f32)
            fade_ref[at, span] = fading * past[:, span]


def local_rows(part, grad, bc, cumul, skip, carried, after, earlier):
    events = grad.shape[0]
    width = grad.shape[1] // PARTS
    blocks = events // GROUP
    at = lambda i: (i, 0)
    step = 4
    return pl.pallas_call(
        functools.partial(local_kernel, part),
        grid=(blocks // step,),
        in_specs=[
            pl.BlockSpec((step * GROUP, width), lambda i: (i, part)),
            pl.BlockSpec((step * GROUP, 2 * STATE), at),
            pl.BlockSpec((step * HEADS, GROUP), at),
            pl.BlockSpec((1, HEADS), lambda i: (0, 0)),
            pl.BlockSpec((step, STATE, width), lambda i: (i, 0, part)),
            pl.BlockSpec((step, 1, width), lambda i: (i, 0, part)),
            pl.BlockSpec(memory_space=pl.ANY),
        ],
        out_specs=[
            pl.BlockSpec((step * GROUP, width), at), pl.BlockSpec((step * GROUP, width), at)
        ],
        out_shape=[
            jax.ShapeDtypeStruct((events, width), f32),
            jax.ShapeDtypeStruct((events, width), f32),
        ],
        compiler_params=params(),
        cost_estimate=cost(
            blocks * GROUP * GROUP * (2 * width + 8 * HEADS), 10 * events * width,
            blocks * GROUP * GROUP * HEADS,
        ),
        name="local",
    )(grad, bc, cumul, skip, carried, after, earlier)


def slots_kernel(owner_ref, row_ref, place_ref, starts_ref, ids_ref):
    holders, _, capacity = ids_ref.shape
    spans = [slice(k * GROUP, (k + 1) * GROUP) for k in range(owner_ref.shape[1] // GROUP)]
    shape = (GROUP, GROUP)
    before = lax.broadcasted_iota(jnp.int32, shape, 0) < lax.broadcasted_iota(jnp.int32, shape, 1)
    before = jnp.where(before, 1.0, 0.0).astype(bf16)
    ones = jnp.ones((8, GROUP), bf16)
    count = jnp.zeros((holders, 1), f32)
    count_row = jnp.zeros((8, holders), f32)
    names = lax.broadcasted_iota(jnp.int32, (holders, GROUP), 0)
    ranks = lax.broadcasted_iota(jnp.int32, (capacity, GROUP), 0)
    high = jnp.zeros((holders, capacity), f32)
    low = jnp.zeros((holders, capacity), f32)
    across = (((1,), (1,)), ((), ()))
    hits_of, rank_of = [], []
    for at in spans:
        hits = jnp.where(names == owner_ref[:, at], 1.0, 0.0)
        hit = hits.astype(bf16)
        earlier = jnp.dot(hit, before, preferred_element_type=f32) + count
        rank = jnp.sum(hits * earlier, axis=0, keepdims=True)
        count = count + jnp.sum(hits, axis=1, keepdims=True)
        count_row = count_row + lax.dot_general(ones, hit, across, preferred_element_type=f32)
        hits_of.append(hits)
        rank_of.append(rank)
        ranked = jnp.where(ranks == rank.astype(jnp.int32), 1.0, 0.0).astype(bf16)
        named = row_ref[:, at] + 1
        upper = (hits * (named // 64).astype(f32)).astype(bf16)
        lower = (hits * (named % 64).astype(f32)).astype(bf16)
        high = high + lax.dot_general(upper, ranked, across, preferred_element_type=f32)
        low = low + lax.dot_general(lower, ranked, across, preferred_element_type=f32)
    ids_ref[:, 0, :] = (high * 64.0 + low).astype(jnp.int32)

    whole = lambda n: jnp.floor((n + (ALIGN - 1)) * (1.0 / ALIGN))
    square = (holders, holders)
    one = lax.broadcasted_iota(jnp.int32, square, 0)
    two = lax.broadcasted_iota(jnp.int32, square, 1)
    column = jnp.broadcast_to(whole(count), (holders, 128)).astype(bf16)
    sooner = jnp.where(two < one, 1.0, 0.0).astype(bf16)
    base = jnp.dot(sooner, column, preferred_element_type=f32)[:, :1] * ALIGN
    sooner = jnp.where(one < two, 1.0, 0.0).astype(bf16)
    starts = jnp.dot(whole(count_row).astype(bf16), sooner, preferred_element_type=f32) * ALIGN
    starts_ref[...] = starts[:1, :].astype(jnp.int32)
    for at, hits, rank in zip(spans, hits_of, rank_of):
        place = jnp.sum(hits * base, axis=0, keepdims=True) + rank
        place_ref[:, at] = place.astype(jnp.int32)


def slots(owner, row, holders, capacity):
    return pl.pallas_call(
        slots_kernel,
        out_shape=[
            jax.ShapeDtypeStruct(owner.shape, jnp.int32),
            jax.ShapeDtypeStruct((1, holders), jnp.int32),
            jax.ShapeDtypeStruct((holders, 1, capacity), jnp.int32),
        ],
        compiler_params=params(),
        cost_estimate=cost(2 * holders * owner.size * (GROUP + 2 * capacity), 8 * owner.size),
        name="slots",
    )(owner, row)


def send_kernel(
    blocks, tiles, sides_ref, starts_ref, place_ref, bc_ref, local_ref, fade_ref, end_ref, *refs,
):
    hops, (_, out_ref, high, low, rows, ordered, done) = refs[:-7], refs[-7:]
    step = pl.program_id(0)
    events, width = rows.shape
    block = events // blocks
    holders = starts_ref.shape[1]
    capacity = out_ref.shape[0] // holders
    tile = (ordered.shape[0] - capacity) // tiles

    @pl.when(step == 0)
    def _():
        state = jnp.zeros((STATE, width), f32)
        for hop in hops[::-1]:
            state = hop[:STATE, :] + jnp.exp(hop[STATE : STATE + 1, :]) * state
        through = end_ref[:STATE, :] + jnp.exp(end_ref[STATE : STATE + 1, :]) * state
        high[...], low[...] = two_parts(jnp.where(sides_ref[0] == 0, through, state))
        ordered[tiles * tile :, :] = jnp.zeros((capacity, width), bf16)

    @pl.when(step < blocks)
    def _():
        b = bc_ref[:, :STATE]
        part = jnp.dot(b, high[...], preferred_element_type=f32) + jnp.dot(
            b, low[...], preferred_element_type=f32
        )
        row = (local_ref[...] + part * fade_ref[...]).astype(bf16)
        rows[pl.ds(pl.multiple_of(step * block, block), block), :] = row

    @pl.when(step >= blocks)
    def _():
        first = pl.multiple_of((step - blocks) * tile, tile)
        names = lax.broadcasted_iota(jnp.int32, (tile, events), 0) + first
        chosen = jnp.where(names == place_ref[...], 1.0, 0.0).astype(bf16)
        ordered[pl.ds(first, tile), :] = jnp.dot(
            chosen, rows[...], preferred_element_type=f32
        ).astype(bf16)

    @pl.when(step == blocks + tiles - 1)
    def _():
        def copy(k):
            start = pl.multiple_of(starts_ref[0, k], ALIGN)
            return pltpu.make_async_copy(
                ordered.at[pl.ds(start, capacity), :],
                out_ref.at[pl.ds(k * capacity, capacity), :],
                done.at[k],
            )

        for k in range(holders):
            copy(k).start()
        for k in range(holders):
            copy(k).wait()


def sent_rows(part, sides, starts, place, bc, local, fade, partner, hops, capacity, earlier):
    events, width = local.shape
    holders = starts.shape[1]
    blocks, tiles = 2, 1
    block = events // blocks
    ordered = -(-(events + (ALIGN - 1) * holders) // (tiles * ALIGN)) * tiles * ALIGN
    whole = lambda a: pl.BlockSpec(a.shape, lambda i: (0,) * a.ndim)
    at = lambda i: (jnp.minimum(i, blocks - 1), 0)
    smem = pl.BlockSpec(memory_space=pltpu.SMEM)
    return pl.pallas_call(
        functools.partial(send_kernel, blocks, tiles),
        grid=(blocks + tiles,),
        in_specs=[
            smem,
            smem,
            whole(place),
            pl.BlockSpec((block, 2 * STATE), at),
            pl.BlockSpec((block, width), at),
            pl.BlockSpec((block, width), at),
        ]
        + [pl.BlockSpec((hop.shape[0], width), lambda i: (0, part)) for hop in (partner, *hops)]
        + [pl.BlockSpec(memory_space=pl.ANY)],
        out_specs=pl.BlockSpec(memory_space=pltpu.HBM),
        out_shape=jax.ShapeDtypeStruct((holders * capacity, width), bf16),
        scratch_shapes=[
            pltpu.VMEM((STATE, width), bf16),
            pltpu.VMEM((STATE, width), bf16),
            pltpu.VMEM((events, width), bf16),
            pltpu.VMEM((ordered + capacity, width), bf16),
            pltpu.SemaphoreType.DMA((holders,)),
        ],
        compiler_params=params(),
        cost_estimate=cost(2 * ordered * events * width, 12 * events * width),
        name="send",
    )(sides, starts, place, bc, local, fade, partner, *hops, earlier)


def update_kernel(tile, ids_ref, got_ref, table_ref, accum_ref, *refs):
    new_table_ref, new_accum_ref = refs[-2:]
    parts, lanes = ids_ref.shape
    ids = jnp.concatenate([ids_ref[k : k + 1, :] for k in range(parts)], axis=1)
    names = lax.broadcasted_iota(jnp.int32, (tile, parts * lanes), 0)
    names = names + (pl.program_id(0) * tile + 1)
    chosen = jnp.where(names == ids, 1.0, 0.0).astype(bf16)
    total = jnp.dot(chosen, got_ref[...], preferred_element_type=f32)
    accum = accum_ref[...] + total * total
    new_accum_ref[...] = accum
    new_table_ref[...] = (
        table_ref[...].astype(f32) - learn_rate * total * lax.rsqrt(accum)
    ).astype(bf16)


def updated(part, ids, got, table, accum, before):
    owned = table.shape[0]
    width = got.shape[1]
    tile = 512
    block = pl.BlockSpec((tile, width), lambda i: (i, part))
    whole = lambda a: pl.BlockSpec(a.shape, lambda i: (0, 0))
    return pl.pallas_call(
        functools.partial(update_kernel, tile),
        grid=(owned // tile,),
        in_specs=[whole(ids), whole(got), block, block]
        + [pl.BlockSpec(memory_space=pl.ANY)] * len(before),
        out_specs=[block] * 2,
        out_shape=[
            jax.ShapeDtypeStruct(table.shape, bf16),
            jax.ShapeDtypeStruct(accum.shape, f32),
        ],
        input_output_aliases={4 + k: k for k in range(len(before))},
        compiler_params=params(60 if part else 40),
        cost_estimate=cost(2 * owned * got.shape[0] * width, 12 * owned * width),
        name="update",
    )(ids, got, table, accum, *before)


def pair_state(side, end, partner):
    early = jnp.where(side == 0, end, partner)
    late = jnp.where(side == 0, partner, end)
    return jnp.concatenate(
        [
            early[:STATE] + jnp.exp(early[STATE : STATE + 1]) * late[:STATE],
            early[STATE:] + late[STATE:],
        ]
    )


def on_device(out_grad, bc_proj, decay_log, skip_gain, owner, item_row, table, accum):
    users, events, width = out_grad.shape
    grad = out_grad.reshape(events, width)
    bc = bc_proj.reshape(events, 2 * STATE)
    decay = decay_log.reshape(HEADS, events)
    size = lax.axis_size("tm")
    holders = size * lax.axis_size("table")
    capacity = 2 * events // holders
    side = lax.axis_index("tm") % 2
    sides = jnp.broadcast_to(side, (1,)).astype(jnp.int32)

    place, starts, ids = slots(owner.reshape(1, events), item_row, holders, capacity)
    got_ids = lax.all_to_all(ids, BOTH, split_axis=0, concat_axis=0, tiled=True)
    ids = got_ids.reshape(-1, 128)
    skip = skip_gain.reshape(1, HEADS)

    carried, after, cumul, end = state_of(grad, bc, decay)
    partner = lax.ppermute(end, "tm", [(i, i ^ 1) for i in range(size)])
    place, partner = lax.optimization_barrier((place, partner))
    pair = pair_state(side, end, partner)
    hops = [
        lax.ppermute(pair, "tm", [(i, i - k) for i in range(k, size)]) for k in range(2, size, 2)
    ]

    new, earlier = (), pair
    for part in range(PARTS):
        local, fade = local_rows(part, grad, bc, cumul, skip, carried, after, earlier)
        rows = sent_rows(
            part, sides, starts, place, bc, local, fade, partner, hops, capacity, got_ids
        )
        got = lax.all_to_all(
            rows.reshape(holders, capacity, -1), BOTH, split_axis=0, concat_axis=0, tiled=True
        )
        new = updated(part, ids, got.reshape(holders * capacity, -1), table, accum, new)
        earlier = rows
    return new


def solution(mesh):
    placed = (
        P("table", "tm", None),
        P("table", "tm", None),
        P("table", None, "tm"),
        P(),
        P("table", "tm", None),
        P("table", "tm"),
        P(("tm", "table"), None),
        P(("tm", "table"), None),
    )
    return jax.shard_map(
        on_device,
        mesh=mesh,
        in_specs=placed,
        out_specs=(P(("tm", "table"), None), P(("tm", "table"), None)),
        check_vma=False,
    )
```

```python
import functools

import jax
import jax.numpy as jnp
from jax import lax
from jax.experimental import pallas as pl
from jax.experimental.pallas import tpu as pltpu
from jax.sharding import PartitionSpec as P

HEADS = 8
STATE = 64
GROUP = 256
ALIGN = 16
PARTS = 2
PART_HEADS = HEADS // PARTS
BOTH = ("tm", "table")
MIB = 1024 * 1024

learn_rate = 1.0

f32 = jnp.float32
bf16 = jnp.bfloat16


def params(mib=60):
    return pltpu.CompilerParams(vmem_limit_bytes=mib * MIB)


def cost(flops, moved, exps=0):
    return pl.CostEstimate(flops=flops, bytes_accessed=moved, transcendentals=exps)


def cumul_rows(decay):
    shape = (GROUP, GROUP)
    upto = lax.broadcasted_iota(jnp.int32, shape, 0) <= lax.broadcasted_iota(jnp.int32, shape, 1)
    upto = jnp.where(upto, 1.0, 0.0).astype(bf16)
    high = decay.astype(bf16)
    rest = decay - high.astype(f32)
    middle = rest.astype(bf16)
    low = (rest - middle.astype(f32)).astype(bf16)
    return (
        jnp.dot(low, upto, preferred_element_type=f32)
        + jnp.dot(middle, upto, preferred_element_type=f32)
        + jnp.dot(high, upto, preferred_element_type=f32)
    )


def two_parts(x):
    high = x.astype(bf16)
    return high, (x - high.astype(f32)).astype(bf16)


def pair_weights(grad):
    low = lax.broadcasted_iota(jnp.int32, grad.shape, 1) < grad.shape[1] // 2
    none = jnp.zeros_like(grad)
    return jnp.concatenate([jnp.where(low, grad, none), jnp.where(low, none, grad)], axis=0)


def state_kernel(
    grad_ref, bc_ref, decay_ref, carried_ref, after_ref, cumul_ref, end_ref
):
    events, width = grad_ref.shape
    blocks = events // GROUP
    two = 2 * width // HEADS
    cumul = cumul_rows(
        jnp.concatenate([decay_ref[:, b * GROUP : (b + 1) * GROUP] for b in range(blocks)], axis=0)
    )
    cumul_ref[...] = cumul
    grown = jnp.exp(cumul)
    low = lax.broadcasted_iota(jnp.int32, (1, two), 1) < two // 2
    state = jnp.zeros((STATE, width), f32)
    log = jnp.zeros((1, width), f32)
    for b in range(blocks - 1, -1, -1):
        at = pl.ds(b * GROUP, GROUP)
        c = jnp.transpose(bc_ref[at, :].astype(f32))[STATE:, :]
        ends, log_end = [], []
        for h in range(0, HEADS, 2):
            high, rest = [], []
            for k in (b * HEADS + h, b * HEADS + h + 1):
                one, other = two_parts(c * grown[k : k + 1, :])
                high.append(one)
                rest.append(other)
            scaled = jnp.concatenate(
                [jnp.concatenate(high, axis=1), jnp.concatenate(rest, axis=1)], axis=0
            )
            grad = grad_ref[at, h // 2 * two : (h // 2 + 1) * two]
            both = jnp.dot(scaled, pair_weights(grad), preferred_element_type=f32)
            ends.append(both[:STATE, :] + both[STATE:, :])
            last = cumul[b * HEADS + h : b * HEADS + h + 2, GROUP - 1 :]
            log_end.append(jnp.where(low, last[:1, :], last[1:, :]))
        carried_ref[b] = state
        after_ref[b] = log
        log_end = jnp.concatenate(log_end, axis=1)
        state = jnp.concatenate(ends, axis=1) + jnp.exp(log_end) * state
        log = log + log_end
    end_ref[:STATE, :] = state
    end_ref[STATE:, :] = jnp.broadcast_to(log, (8, width))


def state_of(grad, bc, decay):
    events, width = grad.shape
    blocks = events // GROUP
    return pl.pallas_call(
        state_kernel,
        out_shape=[
            jax.ShapeDtypeStruct((blocks, STATE, width), f32),
            jax.ShapeDtypeStruct((blocks, 1, width), f32),
            jax.ShapeDtypeStruct((blocks * HEADS, GROUP), f32),
            jax.ShapeDtypeStruct((STATE + 8, width), f32),
        ],
        compiler_params=params(),
        cost_estimate=cost(4 * events * width * STATE, 4 * events * width),
        name="state",
    )(grad, bc, decay)


def local_kernel(
    part, grad_ref, bc_ref, cumul_ref, skip_ref, carried_ref, after_ref, _, out_ref, fade_ref
):
    width = grad_ref.shape[1]
    two = 2 * width // PART_HEADS
    half = GROUP // 2
    shape = (half, half)
    later = lax.broadcasted_iota(jnp.int32, shape, 1) >= lax.broadcasted_iota(jnp.int32, shape, 0)
    low = lax.broadcasted_iota(jnp.int32, (GROUP, two), 1) < two // 2
    rows = cumul_ref[...]
    columns = jnp.transpose(rows)
    for block in range(grad_ref.shape[0] // GROUP):
        at = pl.ds(block * GROUP, GROUP)
        past = jnp.exp(after_ref[block])
        b, c = bc_ref[at, :STATE], bc_ref[at, STATE:]
        scores = lax.dot_general(b, c, (((1,), (1,)), ((), ())), preferred_element_type=f32)
        first = jnp.where(later, scores[:half, :half], 0.0)
        across = scores[:half, half:]
        last = jnp.where(later, scores[half:, half:], 0.0)
        high, rest = two_parts(carried_ref[block])
        carried = jnp.dot(b, high, preferred_element_type=f32) + jnp.dot(
            b, rest, preferred_element_type=f32
        )
        for h in range(0, PART_HEADS, 2):
            head = part * PART_HEADS + h
            span = slice(h // 2 * two, (h // 2 + 1) * two)
            grad = grad_ref[at, span]
            weights = pair_weights(grad)
            upper, lower, wide, ends = [], [], [], []
            for k in (block * HEADS + head, block * HEADS + head + 1):
                row = rows[k : k + 1, :]
                column = jnp.broadcast_to(columns[:, k : k + 1], (GROUP, two))
                near = jnp.exp(jnp.minimum(row[:, :half] - column[:half, :], 0.0)) * first
                far = jnp.exp(row[:, half:] - column[:half, :]) * across
                end = jnp.exp(jnp.minimum(row[:, half:] - column[half:, :], 0.0)) * last
                upper += [near.astype(bf16), far.astype(bf16)]
                lower.append(end.astype(bf16))
                wide.append(row[:, GROUP - 1 :] - column)
            inner = jnp.concatenate(
                [
                    jnp.dot(
                        jnp.concatenate(upper, axis=1), weights, preferred_element_type=f32
                    ),
                    jnp.dot(
                        jnp.concatenate(lower, axis=1),
                        jnp.concatenate([weights[half:GROUP], weights[GROUP + half :]], axis=0),
                        preferred_element_type=f32,
                    ),
                ],
                axis=0,
            )
            fading = jnp.exp(jnp.where(low, wide[0], wide[1]))
            gain = jnp.where(low[:1, :], skip_ref[:, head : head + 1], skip_ref[:, head + 1 : head + 2])
            out_ref[at, span] = inner + carried[:, span] * fading + gain * grad.astype(f32)
            fade_ref[at, span] = fading * past[:, span]


def local_rows(part, grad, bc, cumul, skip, carried, after, earlier):
    events = grad.shape[0]
    width = grad.shape[1] // PARTS
    blocks = events // GROUP
    at = lambda i: (i, 0)
    step = 4
    return pl.pallas_call(
        functools.partial(local_kernel, part),
        grid=(blocks // step,),
        in_specs=[
            pl.BlockSpec((step * GROUP, width), lambda i: (i, part)),
            pl.BlockSpec((step * GROUP, 2 * STATE), at),
            pl.BlockSpec((step * HEADS, GROUP), at),
            pl.BlockSpec((1, HEADS), lambda i: (0, 0)),
            pl.BlockSpec((step, STATE, width), lambda i: (i, 0, part)),
            pl.BlockSpec((step, 1, width), lambda i: (i, 0, part)),
            pl.BlockSpec(memory_space=pl.ANY),
        ],
        out_specs=[
            pl.BlockSpec((step * GROUP, width), at), pl.BlockSpec((step * GROUP, width), at)
        ],
        out_shape=[
            jax.ShapeDtypeStruct((events, width), f32),
            jax.ShapeDtypeStruct((events, width), f32),
        ],
        compiler_params=params(),
        cost_estimate=cost(
            blocks * GROUP * GROUP * (2 * width + 8 * HEADS), 10 * events * width,
            blocks * GROUP * GROUP * HEADS,
        ),
        name="local",
    )(grad, bc, cumul, skip, carried, after, earlier)


def slots_kernel(owner_ref, row_ref, place_ref, starts_ref, ids_ref):
    holders, _, capacity = ids_ref.shape
    spans = [slice(k * GROUP, (k + 1) * GROUP) for k in range(owner_ref.shape[1] // GROUP)]
    shape = (GROUP, GROUP)
    before = lax.broadcasted_iota(jnp.int32, shape, 0) < lax.broadcasted_iota(jnp.int32, shape, 1)
    before = jnp.where(before, 1.0, 0.0).astype(bf16)
    ones = jnp.ones((8, GROUP), bf16)
    count = jnp.zeros((holders, 1), f32)
    count_row = jnp.zeros((8, holders), f32)
    names = lax.broadcasted_iota(jnp.int32, (holders, GROUP), 0)
    ranks = lax.broadcasted_iota(jnp.int32, (capacity, GROUP), 0)
    high = jnp.zeros((holders, capacity), f32)
    low = jnp.zeros((holders, capacity), f32)
    across = (((1,), (1,)), ((), ()))
    hits_of, rank_of = [], []
    for at in spans:
        hits = jnp.where(names == owner_ref[:, at], 1.0, 0.0)
        hit = hits.astype(bf16)
        earlier = jnp.dot(hit, before, preferred_element_type=f32) + count
        rank = jnp.sum(hits * earlier, axis=0, keepdims=True)
        count = count + jnp.sum(hits, axis=1, keepdims=True)
        count_row = count_row + lax.dot_general(ones, hit, across, preferred_element_type=f32)
        hits_of.append(hits)
        rank_of.append(rank)
        ranked = jnp.where(ranks == rank.astype(jnp.int32), 1.0, 0.0).astype(bf16)
        named = row_ref[:, at] + 1
        upper = (hits * (named // 64).astype(f32)).astype(bf16)
        lower = (hits * (named % 64).astype(f32)).astype(bf16)
        high = high + lax.dot_general(upper, ranked, across, preferred_element_type=f32)
        low = low + lax.dot_general(lower, ranked, across, preferred_element_type=f32)
    ids_ref[:, 0, :] = (high * 64.0 + low).astype(jnp.int32)

    whole = lambda n: jnp.floor((n + (ALIGN - 1)) * (1.0 / ALIGN))
    square = (holders, holders)
    one = lax.broadcasted_iota(jnp.int32, square, 0)
    two = lax.broadcasted_iota(jnp.int32, square, 1)
    column = jnp.broadcast_to(whole(count), (holders, 128)).astype(bf16)
    sooner = jnp.where(two < one, 1.0, 0.0).astype(bf16)
    base = jnp.dot(sooner, column, preferred_element_type=f32)[:, :1] * ALIGN
    sooner = jnp.where(one < two, 1.0, 0.0).astype(bf16)
    starts = jnp.dot(whole(count_row).astype(bf16), sooner, preferred_element_type=f32) * ALIGN
    starts_ref[...] = starts[:1, :].astype(jnp.int32)
    for at, hits, rank in zip(spans, hits_of, rank_of):
        place = jnp.sum(hits * base, axis=0, keepdims=True) + rank
        place_ref[:, at] = place.astype(jnp.int32)


def slots(owner, row, holders, capacity):
    return pl.pallas_call(
        slots_kernel,
        out_shape=[
            jax.ShapeDtypeStruct(owner.shape, jnp.int32),
            jax.ShapeDtypeStruct((1, holders), jnp.int32),
            jax.ShapeDtypeStruct((holders, 1, capacity), jnp.int32),
        ],
        compiler_params=params(),
        cost_estimate=cost(2 * holders * owner.size * (GROUP + 2 * capacity), 8 * owner.size),
        name="slots",
    )(owner, row)


def send_kernel(
    blocks, tiles, sides_ref, starts_ref, place_ref, bc_ref, local_ref, fade_ref, end_ref, *refs,
):
    hops, (out_ref, high, low, rows, ordered, done) = refs[:-6], refs[-6:]
    step = pl.program_id(0)
    events, width = rows.shape
    block = events // blocks
    holders = starts_ref.shape[1]
    capacity = out_ref.shape[0] // holders
    tile = (ordered.shape[0] - capacity) // tiles

    @pl.when(step == 0)
    def _():
        state = jnp.zeros((STATE, width), f32)
        for hop in hops[::-1]:
            state = hop[:STATE, :] + jnp.exp(hop[STATE : STATE + 1, :]) * state
        through = end_ref[:STATE, :] + jnp.exp(end_ref[STATE : STATE + 1, :]) * state
        high[...], low[...] = two_parts(jnp.where(sides_ref[0] == 0, through, state))
        ordered[tiles * tile :, :] = jnp.zeros((capacity, width), bf16)

    @pl.when(step < blocks)
    def _():
        b = bc_ref[:, :STATE]
        part = jnp.dot(b, high[...], preferred_element_type=f32) + jnp.dot(
            b, low[...], preferred_element_type=f32
        )
        row = (local_ref[...] + part * fade_ref[...]).astype(bf16)
        rows[pl.ds(pl.multiple_of(step * block, block), block), :] = row

    @pl.when(step >= blocks)
    def _():
        first = pl.multiple_of((step - blocks) * tile, tile)
        names = lax.broadcasted_iota(jnp.int32, (tile, events), 0) + first
        chosen = jnp.where(names == place_ref[...], 1.0, 0.0).astype(bf16)
        ordered[pl.ds(first, tile), :] = jnp.dot(
            chosen, rows[...], preferred_element_type=f32
        ).astype(bf16)

    @pl.when(step == blocks + tiles - 1)
    def _():
        def copy(k):
            start = pl.multiple_of(starts_ref[0, k], ALIGN)
            return pltpu.make_async_copy(
                ordered.at[pl.ds(start, capacity), :],
                out_ref.at[pl.ds(k * capacity, capacity), :],
                done.at[k],
            )

        for k in range(holders):
            copy(k).start()
        for k in range(holders):
            copy(k).wait()


def sent_rows(part, sides, starts, place, bc, local, fade, partner, hops, capacity):
    events, width = local.shape
    holders = starts.shape[1]
    blocks, tiles = 2, 1
    block = events // blocks
    ordered = -(-(events + (ALIGN - 1) * holders) // (tiles * ALIGN)) * tiles * ALIGN
    whole = lambda a: pl.BlockSpec(a.shape, lambda i: (0,) * a.ndim)
    at = lambda i: (jnp.minimum(i, blocks - 1), 0)
    smem = pl.BlockSpec(memory_space=pltpu.SMEM)
    return pl.pallas_call(
        functools.partial(send_kernel, blocks, tiles),
        grid=(blocks + tiles,),
        in_specs=[
            smem,
            smem,
            whole(place),
            pl.BlockSpec((block, 2 * STATE), at),
            pl.BlockSpec((block, width), at),
            pl.BlockSpec((block, width), at),
        ]
        + [pl.BlockSpec((hop.shape[0], width), lambda i: (0, part)) for hop in (partner, *hops)],
        out_specs=pl.BlockSpec(memory_space=pltpu.HBM),
        out_shape=jax.ShapeDtypeStruct((holders * capacity, width), bf16),
        scratch_shapes=[
            pltpu.VMEM((STATE, width), bf16),
            pltpu.VMEM((STATE, width), bf16),
            pltpu.VMEM((events, width), bf16),
            pltpu.VMEM((ordered + capacity, width), bf16),
            pltpu.SemaphoreType.DMA((holders,)),
        ],
        compiler_params=params(),
        cost_estimate=cost(2 * ordered * events * width, 12 * events * width),
        name="send",
    )(sides, starts, place, bc, local, fade, partner, *hops)


def update_kernel(tile, ids_ref, got_ref, table_ref, accum_ref, *refs):
    new_table_ref, new_accum_ref = refs[-2:]
    parts, lanes = ids_ref.shape
    ids = jnp.concatenate([ids_ref[k : k + 1, :] for k in range(parts)], axis=1)
    names = lax.broadcasted_iota(jnp.int32, (tile, parts * lanes), 0)
    names = names + (pl.program_id(0) * tile + 1)
    chosen = jnp.where(names == ids, 1.0, 0.0).astype(bf16)
    total = jnp.dot(chosen, got_ref[...], preferred_element_type=f32)
    accum = accum_ref[...] + total * total
    new_accum_ref[...] = accum
    new_table_ref[...] = (
        table_ref[...].astype(f32) - learn_rate * total * lax.rsqrt(accum)
    ).astype(bf16)


def updated(part, ids, got, table, accum, before):
    owned = table.shape[0]
    width = got.shape[1]
    tile = 512
    block = pl.BlockSpec((tile, width), lambda i: (i, part))
    whole = lambda a: pl.BlockSpec(a.shape, lambda i: (0, 0))
    return pl.pallas_call(
        functools.partial(update_kernel, tile),
        grid=(owned // tile,),
        in_specs=[whole(ids), whole(got), block, block]
        + [pl.BlockSpec(memory_space=pl.ANY)] * len(before),
        out_specs=[block] * 2,
        out_shape=[
            jax.ShapeDtypeStruct(table.shape, bf16),
            jax.ShapeDtypeStruct(accum.shape, f32),
        ],
        input_output_aliases={4 + k: k for k in range(len(before))},
        compiler_params=params(60 if part else 40),
        cost_estimate=cost(2 * owned * got.shape[0] * width, 12 * owned * width),
        name="update",
    )(ids, got, table, accum, *before)


def joined(early, late):
    return jnp.concatenate(
        [
            early[:STATE] + jnp.exp(early[STATE : STATE + 1]) * late[:STATE],
            early[STATE:] + late[STATE:],
        ]
    )


def on_device(out_grad, bc_proj, decay_log, skip_gain, owner, item_row, table, accum):
    users, events, width = out_grad.shape
    grad = out_grad.reshape(events, width)
    bc = bc_proj.reshape(events, 2 * STATE)
    decay = decay_log.reshape(HEADS, events)
    size = lax.axis_size("tm")
    holders = size * lax.axis_size("table")
    capacity = 2 * events // holders
    side = lax.axis_index("tm") % 2
    sides = jnp.broadcast_to(side, (1,)).astype(jnp.int32)

    place, starts, ids = slots(owner.reshape(1, events), item_row, holders, capacity)
    got_ids = lax.all_to_all(ids, BOTH, split_axis=0, concat_axis=0, tiled=True)
    skip = skip_gain.reshape(1, HEADS)

    carried, after, cumul, end = state_of(grad, bc, decay)
    partner = lax.ppermute(end, "tm", [(i, i ^ 1) for i in range(size)])
    place, partner = lax.optimization_barrier((place, partner))
    pair = joined(jnp.where(side == 0, end, partner), jnp.where(side == 0, partner, end))
    of_part = lambda part, earlier: local_rows(
        part, grad, bc, cumul, skip, carried, after, earlier
    )
    first = of_part(0, pair)
    hops, reach, k = [], pair, 2
    while k < size:
        hop = lax.ppermute(reach, "tm", [(i, i - k) for i in range(k, size)])
        if k == 2:
            hop, first = lax.optimization_barrier((hop, first))
        hops.append(hop)
        reach, k = joined(reach, hop), 2 * k

    new, earlier = (), None
    for part in range(PARTS):
        local, fade = of_part(part, earlier) if part else first
        rows = sent_rows(
            part, sides, starts, place, bc, local, fade, partner, hops, capacity
        )
        if part == 0:
            rows, got_ids = lax.optimization_barrier((rows, got_ids))
        got = lax.all_to_all(
            rows.reshape(holders, capacity, -1), BOTH, split_axis=0, concat_axis=0, tiled=True
        )
        new = updated(part, got_ids.reshape(-1, 128), got.reshape(holders * capacity, -1), table, accum, new)
        earlier = rows
    return new


def solution(mesh):
    placed = (
        P("table", "tm", None),
        P("table", "tm", None),
        P("table", None, "tm"),
        P(),
        P("table", "tm", None),
        P("table", "tm"),
        P(("tm", "table"), None),
        P(("tm", "table"), None),
    )
    return jax.shard_map(
        on_device,
        mesh=mesh,
        in_specs=placed,
        out_specs=(P(("tm", "table"), None), P(("tm", "table"), None)),
        check_vma=False,
    )
```

```python
import functools

import jax
import jax.numpy as jnp
from jax import lax
from jax.experimental import pallas as pl
from jax.experimental.pallas import tpu as pltpu
from jax.sharding import PartitionSpec as P

HEADS = 8
STATE = 64
GROUP = 256
ALIGN = 16
PARTS = 2
PART_HEADS = HEADS // PARTS
BOTH = ("tm", "table")
MIB = 1024 * 1024

learn_rate = 1.0

f32 = jnp.float32
bf16 = jnp.bfloat16


def params(mib=60):
    return pltpu.CompilerParams(vmem_limit_bytes=mib * MIB)


def cost(flops, moved, exps=0):
    return pl.CostEstimate(flops=flops, bytes_accessed=moved, transcendentals=exps)


def cumul_rows(decay):
    shape = (GROUP, GROUP)
    upto = lax.broadcasted_iota(jnp.int32, shape, 0) <= lax.broadcasted_iota(jnp.int32, shape, 1)
    upto = jnp.where(upto, 1.0, 0.0).astype(bf16)
    high = decay.astype(bf16)
    rest = decay - high.astype(f32)
    middle = rest.astype(bf16)
    low = (rest - middle.astype(f32)).astype(bf16)
    return (
        jnp.dot(low, upto, preferred_element_type=f32)
        + jnp.dot(middle, upto, preferred_element_type=f32)
        + jnp.dot(high, upto, preferred_element_type=f32)
    )


def two_parts(x):
    high = x.astype(bf16)
    return high, (x - high.astype(f32)).astype(bf16)


def pair_weights(grad):
    low = lax.broadcasted_iota(jnp.int32, grad.shape, 1) < grad.shape[1] // 2
    none = jnp.zeros_like(grad)
    return jnp.concatenate([jnp.where(low, grad, none), jnp.where(low, none, grad)], axis=0)


def state_kernel(
    grad_ref, bc_ref, decay_ref, carried_ref, after_ref, cumul_ref, end_ref
):
    events, width = grad_ref.shape
    blocks = events // GROUP
    two = 2 * width // HEADS
    cumul = cumul_rows(
        jnp.concatenate([decay_ref[:, b * GROUP : (b + 1) * GROUP] for b in range(blocks)], axis=0)
    )
    cumul_ref[...] = cumul
    grown = jnp.exp(cumul)
    low = lax.broadcasted_iota(jnp.int32, (1, two), 1) < two // 2
    state = jnp.zeros((STATE, width), f32)
    log = jnp.zeros((1, width), f32)
    for b in range(blocks - 1, -1, -1):
        at = pl.ds(b * GROUP, GROUP)
        c = jnp.transpose(bc_ref[at, :].astype(f32))[STATE:, :]
        ends, log_end = [], []
        for h in range(0, HEADS, 2):
            high, rest = [], []
            for k in (b * HEADS + h, b * HEADS + h + 1):
                one, other = two_parts(c * grown[k : k + 1, :])
                high.append(one)
                rest.append(other)
            scaled = jnp.concatenate(
                [jnp.concatenate(high, axis=1), jnp.concatenate(rest, axis=1)], axis=0
            )
            grad = grad_ref[at, h // 2 * two : (h // 2 + 1) * two]
            both = jnp.dot(scaled, pair_weights(grad), preferred_element_type=f32)
            ends.append(both[:STATE, :] + both[STATE:, :])
            last = cumul[b * HEADS + h : b * HEADS + h + 2, GROUP - 1 :]
            log_end.append(jnp.where(low, last[:1, :], last[1:, :]))
        carried_ref[b] = state
        after_ref[b] = log
        log_end = jnp.concatenate(log_end, axis=1)
        state = jnp.concatenate(ends, axis=1) + jnp.exp(log_end) * state
        log = log + log_end
    end_ref[:STATE, :] = state
    end_ref[STATE:, :] = jnp.broadcast_to(log, (8, width))


def state_of(grad, bc, decay):
    events, width = grad.shape
    blocks = events // GROUP
    return pl.pallas_call(
        state_kernel,
        out_shape=[
            jax.ShapeDtypeStruct((blocks, STATE, width), f32),
            jax.ShapeDtypeStruct((blocks, 1, width), f32),
            jax.ShapeDtypeStruct((blocks * HEADS, GROUP), f32),
            jax.ShapeDtypeStruct((STATE + 8, width), f32),
        ],
        compiler_params=params(),
        cost_estimate=cost(4 * events * width * STATE, 4 * events * width),
        name="state",
    )(grad, bc, decay)


def local_kernel(
    part, grad_ref, bc_ref, cumul_ref, skip_ref, carried_ref, after_ref, _, out_ref, fade_ref
):
    width = grad_ref.shape[1]
    two = 2 * width // PART_HEADS
    half = GROUP // 2
    shape = (half, half)
    later = lax.broadcasted_iota(jnp.int32, shape, 1) >= lax.broadcasted_iota(jnp.int32, shape, 0)
    low = lax.broadcasted_iota(jnp.int32, (GROUP, two), 1) < two // 2
    rows = cumul_ref[...]
    columns = jnp.transpose(rows)
    for block in range(grad_ref.shape[0] // GROUP):
        at = pl.ds(block * GROUP, GROUP)
        past = jnp.exp(after_ref[block])
        b, c = bc_ref[at, :STATE], bc_ref[at, STATE:]
        scores = lax.dot_general(b, c, (((1,), (1,)), ((), ())), preferred_element_type=f32)
        first = jnp.where(later, scores[:half, :half], 0.0)
        across = scores[:half, half:]
        last = jnp.where(later, scores[half:, half:], 0.0)
        high, rest = two_parts(carried_ref[block])
        carried = jnp.dot(b, high, preferred_element_type=f32) + jnp.dot(
            b, rest, preferred_element_type=f32
        )
        for h in range(0, PART_HEADS, 2):
            head = part * PART_HEADS + h
            span = slice(h // 2 * two, (h // 2 + 1) * two)
            grad = grad_ref[at, span]
            weights = pair_weights(grad)
            upper, lower, wide, ends = [], [], [], []
            for k in (block * HEADS + head, block * HEADS + head + 1):
                row = rows[k : k + 1, :]
                column = jnp.broadcast_to(columns[:, k : k + 1], (GROUP, two))
                near = jnp.exp(jnp.minimum(row[:, :half] - column[:half, :], 0.0)) * first
                far = jnp.exp(row[:, half:] - column[:half, :]) * across
                end = jnp.exp(jnp.minimum(row[:, half:] - column[half:, :], 0.0)) * last
                upper += [near.astype(bf16), far.astype(bf16)]
                lower.append(end.astype(bf16))
                wide.append(row[:, GROUP - 1 :] - column)
            inner = jnp.concatenate(
                [
                    jnp.dot(
                        jnp.concatenate(upper, axis=1), weights, preferred_element_type=f32
                    ),
                    jnp.dot(
                        jnp.concatenate(lower, axis=1),
                        jnp.concatenate([weights[half:GROUP], weights[GROUP + half :]], axis=0),
                        preferred_element_type=f32,
                    ),
                ],
                axis=0,
            )
            fading = jnp.exp(jnp.where(low, wide[0], wide[1]))
            gain = jnp.where(low[:1, :], skip_ref[:, head : head + 1], skip_ref[:, head + 1 : head + 2])
            out_ref[at, span] = inner + carried[:, span] * fading + gain * grad.astype(f32)
            fade_ref[at, span] = fading * past[:, span]


def local_rows(part, grad, bc, cumul, skip, carried, after, earlier):
    events = grad.shape[0]
    width = grad.shape[1] // PARTS
    blocks = events // GROUP
    at = lambda i: (i, 0)
    step = 4
    return pl.pallas_call(
        functools.partial(local_kernel, part),
        grid=(blocks // step,),
        in_specs=[
            pl.BlockSpec((step * GROUP, width), lambda i: (i, part)),
            pl.BlockSpec((step * GROUP, 2 * STATE), at),
            pl.BlockSpec((step * HEADS, GROUP), at),
            pl.BlockSpec((1, HEADS), lambda i: (0, 0)),
            pl.BlockSpec((step, STATE, width), lambda i: (i, 0, part)),
            pl.BlockSpec((step, 1, width), lambda i: (i, 0, part)),
            pl.BlockSpec(memory_space=pl.ANY),
        ],
        out_specs=[
            pl.BlockSpec((step * GROUP, width), at), pl.BlockSpec((step * GROUP, width), at)
        ],
        out_shape=[
            jax.ShapeDtypeStruct((events, width), f32),
            jax.ShapeDtypeStruct((events, width), f32),
        ],
        compiler_params=params(),
        cost_estimate=cost(
            blocks * GROUP * GROUP * (2 * width + 8 * HEADS), 10 * events * width,
            blocks * GROUP * GROUP * HEADS,
        ),
        name="local",
    )(grad, bc, cumul, skip, carried, after, earlier)


def slots_kernel(owner_ref, row_ref, place_ref, starts_ref, ids_ref):
    holders, _, capacity = ids_ref.shape
    spans = [slice(k * GROUP, (k + 1) * GROUP) for k in range(owner_ref.shape[1] // GROUP)]
    shape = (GROUP, GROUP)
    before = lax.broadcasted_iota(jnp.int32, shape, 0) < lax.broadcasted_iota(jnp.int32, shape, 1)
    before = jnp.where(before, 1.0, 0.0).astype(bf16)
    ones = jnp.ones((8, GROUP), bf16)
    count = jnp.zeros((holders, 1), f32)
    count_row = jnp.zeros((8, holders), f32)
    names = lax.broadcasted_iota(jnp.int32, (holders, GROUP), 0)
    ranks = lax.broadcasted_iota(jnp.int32, (capacity, GROUP), 0)
    high = jnp.zeros((holders, capacity), f32)
    low = jnp.zeros((holders, capacity), f32)
    across = (((1,), (1,)), ((), ()))
    hits_of, rank_of = [], []
    for at in spans:
        hits = jnp.where(names == owner_ref[:, at], 1.0, 0.0)
        hit = hits.astype(bf16)
        earlier = jnp.dot(hit, before, preferred_element_type=f32) + count
        rank = jnp.sum(hits * earlier, axis=0, keepdims=True)
        count = count + jnp.sum(hits, axis=1, keepdims=True)
        count_row = count_row + lax.dot_general(ones, hit, across, preferred_element_type=f32)
        hits_of.append(hits)
        rank_of.append(rank)
        ranked = jnp.where(ranks == rank.astype(jnp.int32), 1.0, 0.0).astype(bf16)
        named = row_ref[:, at] + 1
        upper = (hits * (named // 64).astype(f32)).astype(bf16)
        lower = (hits * (named % 64).astype(f32)).astype(bf16)
        high = high + lax.dot_general(upper, ranked, across, preferred_element_type=f32)
        low = low + lax.dot_general(lower, ranked, across, preferred_element_type=f32)
    ids_ref[:, 0, :] = (high * 64.0 + low).astype(jnp.int32)

    whole = lambda n: jnp.floor((n + (ALIGN - 1)) * (1.0 / ALIGN))
    square = (holders, holders)
    one = lax.broadcasted_iota(jnp.int32, square, 0)
    two = lax.broadcasted_iota(jnp.int32, square, 1)
    column = jnp.broadcast_to(whole(count), (holders, 128)).astype(bf16)
    sooner = jnp.where(two < one, 1.0, 0.0).astype(bf16)
    base = jnp.dot(sooner, column, preferred_element_type=f32)[:, :1] * ALIGN
    sooner = jnp.where(one < two, 1.0, 0.0).astype(bf16)
    starts = jnp.dot(whole(count_row).astype(bf16), sooner, preferred_element_type=f32) * ALIGN
    starts_ref[...] = starts[:1, :].astype(jnp.int32)
    for at, hits, rank in zip(spans, hits_of, rank_of):
        place = jnp.sum(hits * base, axis=0, keepdims=True) + rank
        place_ref[:, at] = place.astype(jnp.int32)


def slots(owner, row, holders, capacity):
    return pl.pallas_call(
        slots_kernel,
        out_shape=[
            jax.ShapeDtypeStruct(owner.shape, jnp.int32),
            jax.ShapeDtypeStruct((1, holders), jnp.int32),
            jax.ShapeDtypeStruct((holders, 1, capacity), jnp.int32),
        ],
        compiler_params=params(),
        cost_estimate=cost(2 * holders * owner.size * (GROUP + 2 * capacity), 8 * owner.size),
        name="slots",
    )(owner, row)


def send_kernel(
    blocks, tiles, sides_ref, starts_ref, place_ref, bc_ref, local_ref, fade_ref, end_ref, *refs,
):
    hops, (out_ref, high, low, rows, ordered, done) = refs[:-6], refs[-6:]
    step = pl.program_id(0)
    events, width = rows.shape
    block = events // blocks
    holders = starts_ref.shape[1]
    capacity = out_ref.shape[0] // holders
    tile = (ordered.shape[0] - capacity) // tiles

    @pl.when(step == 0)
    def _():
        state = jnp.zeros((STATE, width), f32)
        for hop in hops[::-1]:
            state = hop[:STATE, :] + jnp.exp(hop[STATE : STATE + 1, :]) * state
        through = end_ref[:STATE, :] + jnp.exp(end_ref[STATE : STATE + 1, :]) * state
        high[...], low[...] = two_parts(jnp.where(sides_ref[0] == 0, through, state))
        ordered[tiles * tile :, :] = jnp.zeros((capacity, width), bf16)

    @pl.when(step < blocks)
    def _():
        b = bc_ref[:, :STATE]
        part = jnp.dot(b, high[...], preferred_element_type=f32) + jnp.dot(
            b, low[...], preferred_element_type=f32
        )
        row = (local_ref[...] + part * fade_ref[...]).astype(bf16)
        rows[pl.ds(pl.multiple_of(step * block, block), block), :] = row

    @pl.when(step >= blocks)
    def _():
        first = pl.multiple_of((step - blocks) * tile, tile)
        names = lax.broadcasted_iota(jnp.int32, (tile, events), 0) + first
        chosen = jnp.where(names == place_ref[...], 1.0, 0.0).astype(bf16)
        ordered[pl.ds(first, tile), :] = jnp.dot(
            chosen, rows[...], preferred_element_type=f32
        ).astype(bf16)

    @pl.when(step == blocks + tiles - 1)
    def _():
        def copy(k):
            start = pl.multiple_of(starts_ref[0, k], ALIGN)
            return pltpu.make_async_copy(
                ordered.at[pl.ds(start, capacity), :],
                out_ref.at[pl.ds(k * capacity, capacity), :],
                done.at[k],
            )

        for k in range(holders):
            copy(k).start()
        for k in range(holders):
            copy(k).wait()


def sent_rows(part, sides, starts, place, bc, local, fade, partner, hops, capacity):
    events, width = local.shape
    holders = starts.shape[1]
    blocks, tiles = 2, 1
    block = events // blocks
    ordered = -(-(events + (ALIGN - 1) * holders) // (tiles * ALIGN)) * tiles * ALIGN
    whole = lambda a: pl.BlockSpec(a.shape, lambda i: (0,) * a.ndim)
    at = lambda i: (jnp.minimum(i, blocks - 1), 0)
    smem = pl.BlockSpec(memory_space=pltpu.SMEM)
    return pl.pallas_call(
        functools.partial(send_kernel, blocks, tiles),
        grid=(blocks + tiles,),
        in_specs=[
            smem,
            smem,
            whole(place),
            pl.BlockSpec((block, 2 * STATE), at),
            pl.BlockSpec((block, width), at),
            pl.BlockSpec((block, width), at),
        ]
        + [pl.BlockSpec((hop.shape[0], width), lambda i: (0, part)) for hop in (partner, *hops)],
        out_specs=pl.BlockSpec(memory_space=pltpu.HBM),
        out_shape=jax.ShapeDtypeStruct((holders * capacity, width), bf16),
        scratch_shapes=[
            pltpu.VMEM((STATE, width), bf16),
            pltpu.VMEM((STATE, width), bf16),
            pltpu.VMEM((events, width), bf16),
            pltpu.VMEM((ordered + capacity, width), bf16),
            pltpu.SemaphoreType.DMA((holders,)),
        ],
        compiler_params=params(58),
        cost_estimate=cost(2 * ordered * events * width, 12 * events * width),
        name="send",
    )(sides, starts, place, bc, local, fade, partner, *hops)


def update_kernel(tile, ids_ref, got_ref, table_ref, accum_ref, *refs):
    new_table_ref, new_accum_ref = refs[-2:]
    parts, lanes = ids_ref.shape
    ids = jnp.concatenate([ids_ref[k : k + 1, :] for k in range(parts)], axis=1)
    names = lax.broadcasted_iota(jnp.int32, (tile, parts * lanes), 0)
    names = names + (pl.program_id(0) * tile + 1)
    chosen = jnp.where(names == ids, 1.0, 0.0).astype(bf16)
    total = jnp.dot(chosen, got_ref[...], preferred_element_type=f32)
    accum = accum_ref[...] + total * total
    new_accum_ref[...] = accum
    new_table_ref[...] = (
        table_ref[...].astype(f32) - learn_rate * total * lax.rsqrt(accum)
    ).astype(bf16)


def updated(part, ids, got, table, accum, before):
    owned = table.shape[0]
    width = got.shape[1]
    tile = 512
    block = pl.BlockSpec((tile, width), lambda i: (i, part))
    whole = lambda a: pl.BlockSpec(a.shape, lambda i: (0, 0))
    return pl.pallas_call(
        functools.partial(update_kernel, tile),
        grid=(owned // tile,),
        in_specs=[whole(ids), whole(got), block, block]
        + [pl.BlockSpec(memory_space=pl.ANY)] * len(before),
        out_specs=[block] * 2,
        out_shape=[
            jax.ShapeDtypeStruct(table.shape, bf16),
            jax.ShapeDtypeStruct(accum.shape, f32),
        ],
        input_output_aliases={4 + k: k for k in range(len(before))},
        compiler_params=params(60 if part else 40),
        cost_estimate=cost(2 * owned * got.shape[0] * width, 12 * owned * width),
        name="update",
    )(ids, got, table, accum, *before)


def joined(early, late):
    return jnp.concatenate(
        [
            early[:STATE] + jnp.exp(early[STATE : STATE + 1]) * late[:STATE],
            early[STATE:] + late[STATE:],
        ]
    )


def on_device(out_grad, bc_proj, decay_log, skip_gain, owner, item_row, table, accum):
    users, events, width = out_grad.shape
    grad = out_grad.reshape(events, width)
    bc = bc_proj.reshape(events, 2 * STATE)
    decay = decay_log.reshape(HEADS, events)
    size = lax.axis_size("tm")
    holders = size * lax.axis_size("table")
    capacity = 2 * events // holders
    side = lax.axis_index("tm") % 2
    sides = jnp.broadcast_to(side, (1,)).astype(jnp.int32)

    place, starts, ids = slots(owner.reshape(1, events), item_row, holders, capacity)
    got_ids = lax.all_to_all(ids, BOTH, split_axis=0, concat_axis=0, tiled=True)
    skip = skip_gain.reshape(1, HEADS)

    carried, after, cumul, end = state_of(grad, bc, decay)
    partner = lax.ppermute(end, "tm", [(i, i ^ 1) for i in range(size)])
    place, partner = lax.optimization_barrier((place, partner))
    pair = joined(jnp.where(side == 0, end, partner), jnp.where(side == 0, partner, end))
    of_part = lambda part, earlier: local_rows(
        part, grad, bc, cumul, skip, carried, after, earlier
    )
    first = of_part(0, pair)
    hops, reach, k = [], pair, 2
    while k < size:
        hop = lax.ppermute(reach, "tm", [(i, i - k) for i in range(k, size)])
        if k == 2:
            hop, first = lax.optimization_barrier((hop, first))
        hops.append(hop)
        reach, k = joined(reach, hop), 2 * k

    new, earlier = (), None
    for part in range(PARTS):
        local, fade = of_part(part, earlier) if part else first
        rows = sent_rows(
            part, sides, starts, place, bc, local, fade, partner, hops, capacity
        )
        if part == 0:
            rows, got_ids = lax.optimization_barrier((rows, got_ids))
        got = lax.all_to_all(
            rows.reshape(holders, capacity, -1), BOTH, split_axis=0, concat_axis=0, tiled=True
        )
        new = updated(part, got_ids.reshape(-1, 128), got.reshape(holders * capacity, -1), table, accum, new)
        earlier = rows
    return new


def solution(mesh):
    placed = (
        P("table", "tm", None),
        P("table", "tm", None),
        P("table", None, "tm"),
        P(),
        P("table", "tm", None),
        P("table", "tm"),
        P(("tm", "table"), None),
        P(("tm", "table"), None),
    )
    return jax.shard_map(
        on_device,
        mesh=mesh,
        in_specs=placed,
        out_specs=(P(("tm", "table"), None), P(("tm", "table"), None)),
        check_vma=False,
    )
```
